256 devices in a mesh: seq: 64 (over y, x_lo, z), rep: 4 (over x_hi, core).
Axes of the slice: x: 4 (x_hi: 2, x_lo: 2; x = x_hi * 2 + x_lo), y: 4, z: 8, core: 2. Of those that a mesh axis runs over, the one named last changes fastest.
Arguments:
- inputs: bfloat16 [4, 4, 4096, 1024], P('rep', None, 'seq'), may hold values from -16 to 16
- upstream: bfloat16 [4, 4, 4096, 1024], P('rep', None, 'seq'), may hold values from -6 to 6
- qkv_weight: bfloat16 [1024, 3072], P(None, 'rep'), may hold values from -1 to 1
- out_weight: bfloat16 [1024, 1024], P(None, 'rep'), may hold values from -0.1875 to 0.1875
Outputs:
- input_grad: bfloat16 [4, 4, 4096, 1024], P('rep', None, 'seq')
- qkv_grad: float32 [1024, 3072], P('seq', 'rep')
- out_grad: float32 [1024, 1024], P('seq', 'rep')
The draws below stay inside these ranges and needn't reach their ends.
All inputs are finite; a program needn't handle non-finite values.
Results may differ from the reference program's by a relative error of at most 0.022.
The reference program's roundings to bfloat16 on the way count: a program that leaves them out, or rounds other values in their place, can miss the bound.
Values may be sent and summed in bfloat16 or wider, within the bound.
No kernel may reach another device: no remote copies, remote signals or barrier semaphores. Data moves between devices by JAX's collectives and lax.ppermute only.
A program may use at most 128 MiB of HBM per device.

```python
import math
import jax
import jax.numpy as jnp
from jax import lax

D = 1024
HEADS = 16
HD = 64
SEQS = 4
ATT = 1024
REPLICAS = 4
LEN = 4096
WINDOW = 512


def draw_qkv_weight(key, part):
    width = HEADS * HD
    base = jax.random.normal(key, (D, 3 * width), jnp.float32) / math.sqrt(D)
    return jnp.clip(base, -1.0, 1.0).astype(jnp.bfloat16)


def raised(array, rng, source, target, parts, factor):
    owner, partner = [(jnp.arange(array.shape[dim]) // (array.shape[dim] // parts)).reshape([-1 if axis == dim else 1 for axis in range(array.ndim)]) for dim in (source, target)]
    chosen = jax.random.permutation(rng, parts)[partner]
    strong = (owner == chosen) | (owner == (partner + parts // 2) % parts)
    return jnp.where(strong, factor * array, array)


def block_levels(own_key, shape, pieces, least, largest):
    level = 1.0
    for dim, parts in pieces:
        draws = jax.random.uniform(jax.random.fold_in(jax.random.fold_in(own_key, 6), dim), (parts,), jnp.float32, least / len(pieces), largest / len(pieces))
        level = level * jnp.repeat(jnp.exp(draws), shape[dim] // parts).reshape((-1,) + (1,) * (len(shape) - 1 - dim))
    return level


def bell_draw(key, dims, spread, limit, shards=(), kind=jnp.bfloat16):
    values = jax.random.normal(key, dims, jnp.float32) * spread
    if len(shards) > 0:
        values = block_levels(key, dims, shards, -0.22, 0.18) * values
    return jnp.clip(values, min=-limit, max=limit).astype(kind)


def gaussian_with(key, extent, scale, bound, split, heavy, held_as=jnp.bfloat16):
    drawn = scale * jax.random.normal(key, extent, jnp.float32)
    if split:
        drawn = drawn * block_levels(key, extent, split, -0.22, 0.18)
    return jnp.clip(raised(drawn, jax.random.fold_in(key, 3), *heavy), -bound, bound).astype(held_as)


def setup_inputs(seed: int = 0) -> dict:
    key_of = jax.random.split(jax.random.key(seed), 5)
    inputs = gaussian_with(key_of[0], (REPLICAS, SEQS, LEN, D), 1.0, 16.0, ((0, 4), (2, 64)), (2, 3, 64, 4.0))
    upstream = gaussian_with(key_of[1], (REPLICAS, SEQS, LEN, D), 1.0, 6.0, ((0, 4), (2, 64)), (0, 3, 4, 2.0))
    qkv_weight = draw_qkv_weight(jax.random.fold_in(key_of[4], 71), 0)
    out_weight = bell_draw(key_of[3], (ATT, D), ATT ** -0.5, 0.1875, ((1, 4),))
    return {"inputs": inputs, "upstream": upstream, "qkv_weight": qkv_weight, "out_weight": out_weight}


def attend_item(packed):
    query, keys, values, cot = packed
    scaling = HD ** -0.5
    length = query.shape[0]
    width = query.shape[1]
    block_rows = min(512, length)
    slab_len = WINDOW + block_rows
    pad_rows = jnp.zeros((WINDOW, width), keys.dtype)
    keys_pad = jnp.concatenate([pad_rows, keys], axis=0)
    values_pad = jnp.concatenate([pad_rows, values], axis=0)

    def one_block(totals, block_index):
        key_total, value_total = totals
        offset = (block_index * block_rows).astype(jnp.int32)
        query_block = lax.dynamic_slice_in_dim(query, offset, block_rows, 0)
        cot_block = lax.dynamic_slice_in_dim(cot, offset, block_rows, 0)
        key_slab = lax.dynamic_slice_in_dim(keys_pad, offset, slab_len, 0)
        value_slab = lax.dynamic_slice_in_dim(values_pad, offset, slab_len, 0)
        scores = jnp.dot(query_block.astype(jnp.float32), key_slab.astype(jnp.float32).T) * scaling
        row_pos = offset + jnp.arange(block_rows, dtype=jnp.int32)[:, None]
        col_pos = offset - WINDOW + jnp.arange(slab_len, dtype=jnp.int32)[None, :]
        allowed = (col_pos <= row_pos) & (row_pos - col_pos < WINDOW) & (col_pos >= 0)
        scores = jnp.where(allowed, scores, -jnp.inf)
        highest = jnp.max(scores, axis=1, keepdims=True)
        weights = jnp.exp(scores - highest)
        probs = weights / jnp.sum(weights, axis=1, keepdims=True)
        probs_low = probs.astype(jnp.bfloat16)
        attended = jnp.dot(probs_low, value_slab, preferred_element_type=jnp.float32)
        delta = jnp.sum(cot_block.astype(jnp.float32) * attended, axis=1, keepdims=True)
        prob_grad = jnp.dot(cot_block, value_slab.T, preferred_element_type=jnp.float32)
        score_grad = (probs * (prob_grad - delta)).astype(jnp.bfloat16)
        query_grad = (jnp.dot(score_grad, key_slab, preferred_element_type=jnp.float32) * scaling).astype(jnp.bfloat16)
        key_part = jnp.dot(score_grad.T, query_block, preferred_element_type=jnp.float32)
        value_part = jnp.dot(probs_low.T, cot_block, preferred_element_type=jnp.float32)
        key_total = lax.dynamic_update_slice_in_dim(key_total, lax.dynamic_slice_in_dim(key_total, offset, slab_len, 0) + key_part, offset, 0)
        value_total = lax.dynamic_update_slice_in_dim(value_total, lax.dynamic_slice_in_dim(value_total, offset, slab_len, 0) + value_part, offset, 0)
        return (key_total, value_total), (query_grad, attended.astype(jnp.bfloat16))

    zeros_init = jnp.zeros((WINDOW + length, width), jnp.float32)
    totals, blocks = lax.scan(one_block, (zeros_init, zeros_init), jnp.arange(length // block_rows, dtype=jnp.int32))
    query_grad = blocks[0].reshape(length, width)
    attended_reduced_precision = blocks[1].reshape(length, width)
    key_grad = (totals[0][WINDOW:] * scaling).astype(jnp.bfloat16)
    value_grad = totals[1][WINDOW:].astype(jnp.bfloat16)
    return query_grad, key_grad, value_grad, attended_reduced_precision


def reference(inputs, upstream, qkv_weight, out_weight):
    weight_quadruple = qkv_weight.reshape(D, 3, HEADS, HD).astype(jnp.float32)
    output_triple = out_weight.reshape(HEADS, HD, D).astype(jnp.float32)
    input_gradient_rows = []
    query_key_value_total = jnp.zeros((D, 3, HEADS, HD), jnp.float32)
    output_grand_total = jnp.zeros((HEADS, HD, D), jnp.float32)
    for replica in range(REPLICAS):
        source_tensor = inputs[replica].astype(jnp.float32)
        incoming_cotangent = upstream[replica].astype(jnp.float32)
        projected_rows = jnp.einsum('uvj,jrxb->ruxvb', source_tensor, weight_quadruple).astype(jnp.bfloat16)
        output_cotangent = jnp.einsum('kwc,ipc->kiwp', incoming_cotangent, output_triple).astype(jnp.bfloat16)
        flat_shape = (SEQS * HEADS, LEN, HD)
        results = lax.map(attend_item, (projected_rows[0].reshape(flat_shape), projected_rows[1].reshape(flat_shape), projected_rows[2].reshape(flat_shape), output_cotangent.reshape(flat_shape)))
        item_shape = (SEQS, HEADS, LEN, HD)
        projection_gradient = jnp.stack([results[0].reshape(item_shape), results[1].reshape(item_shape), results[2].reshape(item_shape)], axis=0).astype(jnp.float32)
        attended_reduced_precision = results[3].reshape(item_shape).astype(jnp.float32)
        input_gradient_rows.append(jnp.einsum('jtkum,zjkm->tuz', projection_gradient, weight_quadruple).astype(jnp.bfloat16))
        query_key_value_total = query_key_value_total + jnp.einsum('xra,zxfrj->azfj', source_tensor, projection_gradient)
        output_grand_total = output_grand_total + jnp.einsum('vpxi,vxo->pio', attended_reduced_precision, incoming_cotangent)
    input_grad = jnp.stack(input_gradient_rows, axis=0)
    return input_grad, query_key_value_total.reshape(D, 3 * HEADS * HD), output_grand_total.reshape(HEADS * HD, D)
```

```python
import functools

import jax
import jax.numpy as jnp
from jax import lax
from jax.experimental import pallas as pl
from jax.experimental.pallas import tpu as pltpu
from jax.sharding import PartitionSpec as P

D = 1024
HEADS = 16
HD = 64
WINDOW = 512
NY, NX, NZ = 4, 4, 8
BOTH = ("seq", "rep")
BF16 = jnp.bfloat16
F32 = jnp.float32
LOG2E = 1.4426950408889634


def flat(y, x, z, c):
    y, x, z = y % NY, x % NX, z % NZ
    return ((y * 2 + x % 2) * NZ + z) * 4 + (x // 2) * 2 + c


PLACES = [(y, x, z, c) for y in range(NY) for x in range(NX) for z in range(NZ) for c in range(2)]


def move(value, target):
    pairs = []
    for place in PLACES:
        goal = target(*place)
        if goal is not None:
            pairs.append((flat(*place), flat(*goal)))
    return lax.ppermute(value, BOTH, pairs)


def other_core(value):
    return move(value, lambda y, x, z, c: (y, x, z, 1 - c))


def mm(a, b, ca, cb):
    return lax.dot_general(a, b, (((ca,), (cb,)), ((), ())), preferred_element_type=F32)


def attention_kernel(bias_ref, q_ref, g_ref, kh_ref, ko_ref, vh_ref, vo_ref,
                     dq_ref, att_ref, dkh_ref, dko_ref, dvh_ref, dvo_ref):
    size = 256
    bias = bias_ref[0, 0]
    low = lax.broadcasted_iota(jnp.int32, (1, 2 * HD), 1) < HD
    upper = (
        lax.broadcasted_iota(jnp.int32, (size, size), 0) > lax.broadcasted_iota(jnp.int32, (size, size), 1)
    )
    factor = LOG2E * HD ** -0.5

    def part(halo, own, index):
        ref, at = (halo, index) if index < 2 else (own, index - 2)
        return ref[at * size:(at + 1) * size, :]

    keys = [part(kh_ref, ko_ref, i) for i in range(4)]
    vals = [part(vh_ref, vo_ref, i) for i in range(4)]
    keys_t = [k.T for k in keys]
    vals_t = [v.T for v in vals]
    dk = [None] * 4
    dv = [None] * 4

    def add(total, index, term):
        total[index] = term if total[index] is None else total[index] + term

    for block in range(2):
        rows = slice(block * size, (block + 1) * size)
        q_pair = q_ref[rows, :]
        g_pair = g_ref[rows, :]
        g_t = g_pair.T.astype(F32)
        dq_t = []
        for head in range(2):
            mine = low if head == 0 else jnp.logical_not(low)
            lanes = slice(head * HD, (head + 1) * HD)
            q = jnp.where(mine, q_pair, jnp.zeros_like(q_pair))
            g = jnp.where(mine, g_pair, jnp.zeros_like(g_pair))
            s0, s1, s2 = [mm(keys[block + i], q, 1, 1) for i in range(3)]
            edge = jnp.where(upper, s0 + bias, s2)
            if block == 0:
                s1 = s1 + bias
            top = jnp.maximum(
                jnp.max(edge, axis=0, keepdims=True), jnp.max(s1, axis=0, keepdims=True)
            )
            edge = jnp.exp2((edge - top) * factor)
            full = jnp.exp2((s1 - top) * factor)
            scale = 1.0 / (jnp.sum(edge, axis=0, keepdims=True) + jnp.sum(full, axis=0, keepdims=True))
            edge = edge * scale
            full = full * scale
            p0 = jnp.where(upper, edge, 0.0).astype(BF16)
            p1 = full.astype(BF16)
            p2 = jnp.where(upper, 0.0, edge).astype(BF16)
            att = (
                mm(vals_t[block][lanes], p0, 1, 0)
                + mm(vals_t[block + 1][lanes], p1, 1, 0)
                + mm(vals_t[block + 2][lanes], p2, 1, 0)
            )
            delta = jnp.sum(g_t[lanes] * att, axis=0, keepdims=True)
            att_ref[lanes, rows] = att.astype(BF16)
            d0, d1, d2 = [mm(vals[block + i], g, 1, 1) for i in range(3)]
            d_edge = edge * (jnp.where(upper, d0, d2) - delta)
            z0 = jnp.where(upper, d_edge, 0.0).astype(BF16)
            z1 = (full * (d1 - delta)).astype(BF16)
            z2 = jnp.where(upper, 0.0, d_edge).astype(BF16)
            dq_t.append(
                mm(keys_t[block][lanes], z0, 1, 0)
                + mm(keys_t[block + 1][lanes], z1, 1, 0)
                + mm(keys_t[block + 2][lanes], z2, 1, 0)
            )
            for i, (p, z) in enumerate(((p0, z0), (p1, z1), (p2, z2))):
                add(dv, block + i, mm(p, g, 1, 0))
                add(dk, block + i, mm(z, q, 1, 0))
        dq = jnp.concatenate(dq_t, axis=0) * (HD ** -0.5)
        dq_ref[rows, :] = dq.T.astype(BF16)
    for i in range(4):
        at = slice((i % 2) * size, (i % 2 + 1) * size)
        (dkh_ref if i < 2 else dko_ref)[at, :] = (dk[i] * (HD ** -0.5)).astype(BF16)
        (dvh_ref if i < 2 else dvo_ref)[at, :] = dv[i].astype(BF16)


def attention(bias, qkv, halo_kv, g):
    tokens, width = g.shape
    pairs = width // (2 * HD)

    def cols(first):
        return pl.BlockSpec((tokens, 2 * HD), lambda i, first=first: (0, first + i))

    block = cols(0)
    like = jax.ShapeDtypeStruct((tokens, width), BF16)
    return pl.pallas_call(
        attention_kernel,
        grid=(pairs,),
        in_specs=[
            pl.BlockSpec(memory_space=pltpu.SMEM),
            cols(0),
            block,
            cols(0),
            cols(pairs),
            cols(pairs),
            cols(2 * pairs),
        ],
        out_specs=[block, pl.BlockSpec((2 * HD, tokens), lambda i: (i, 0)), block, block, block, block],
        out_shape=[like, jax.ShapeDtypeStruct((width, tokens), BF16), like, like, like, like],
        compiler_params=pltpu.CompilerParams(vmem_limit_bytes=48 * 1024 * 1024),
        cost_estimate=pl.CostEstimate(
            flops=16 * 768 * 256 * 64 * 12, bytes_accessed=6 * 1024 * 1024, transcendentals=16 * 512 * 256
        ),
    )(bias, qkv, g, halo_kv, qkv, halo_kv, qkv)


def spread_sum(value, here, size, target):
    total = lax.dynamic_index_in_dim(value, here, 0, keepdims=False).astype(F32)
    for step in range(1, size):
        chunk = lax.dynamic_index_in_dim(value, lax.rem(here + step, size), 0, keepdims=False)
        total = total + move(chunk, functools.partial(target, step)).astype(F32)
    return total


def along_y(step, y, x, z, c):
    return (y + step, x, z, c)


def along_x(step, y, x, z, c):
    return (y, x + step, z, c)


def along_z(step, y, x, z, c):
    return (y, x, z + step, c)


Z_GROUPS = [[ring * NZ + z for z in range(NZ)] for ring in range(8)]


def body(inputs, upstream, qkv_weight, out_weight):
    at = lax.axis_index("seq")
    rep = lax.axis_index("rep")
    core = lax.rem(rep, 2)
    x_hi = rep // 2
    z = lax.rem(at, NZ)
    ring = at // NZ
    y = ring // 2
    x = x_hi * 2 + lax.rem(ring, 2)
    first = core == 0

    shard = jnp.concatenate([qkv_weight, out_weight], axis=1)
    far = move(shard, lambda y, x, z, c: (y, 3 - x, z, c))

    a, b = inputs[0], upstream[0]
    kept = jnp.where(first, a, b)
    came = other_core(jnp.where(first, b, a))
    mixed = jnp.concatenate([jnp.where(first, kept, came), jnp.where(first, came, kept)], axis=0)
    gathered = lax.all_to_all(mixed, "seq", 0, 0, axis_index_groups=Z_GROUPS, tiled=True)
    gathered = gathered.reshape(NZ * 64, D)
    swapped = other_core(gathered)
    src = jnp.where(first, gathered, swapped)
    cot = jnp.where(first, swapped, gathered)

    def next_ring(y, x, z, c):
        ring = 2 * y + x % 2 + 1
        return None if ring == 8 else (ring // 2, (x // 2) * 2 + ring % 2, z, c)

    def last_ring(y, x, z, c):
        ring = 2 * y + x % 2 - 1
        return None if ring < 0 else (ring // 2, (x // 2) * 2 + ring % 2, z, c)

    half = lax.dynamic_slice_in_dim(src, core * 256, 256, 0)
    halo = move(half, next_ring)
    halo_other = other_core(halo)
    halo = jnp.concatenate(
        [jnp.where(first, halo, halo_other), jnp.where(first, halo_other, halo)], axis=0
    )

    lo = jnp.where(x_hi == 0, shard, far)
    hi = jnp.where(x_hi == 0, far, shard)
    lo_w, lo_o, hi_w, hi_o = lo[:, :768], lo[:, 768:], hi[:, :768], hi[:, 768:]
    send = jnp.concatenate(
        [
            jnp.where(first, lo_w[:, 512:], hi_w[:, :256]),
            jnp.where(first, hi_w[:, :512], lo_w[:, 256:]),
        ],
        axis=1,
    )
    got = other_core(send)
    got256, got512 = got[:, :256], got[:, 256:]
    weight = jnp.concatenate(
        [
            jnp.where(first, lo_w[:, :256], got256),
            jnp.where(first, lo_w[:, 256:512], lo_w[:, :256]),
            got512,
            jnp.where(first, hi_w[:, 512:], hi_w[:, 256:512]),
            jnp.where(first, got256, hi_w[:, 512:]),
        ],
        axis=1,
    )
    pair_o = jnp.stack([lo_o, hi_o], axis=0)
    keep_o = lax.dynamic_slice_in_dim(pair_o, core * 512, 512, 1)
    got_o = other_core(lax.dynamic_slice_in_dim(pair_o, (1 - core) * 512, 512, 1))
    weight_o = jnp.concatenate(
        [
            jnp.where(first, keep_o[0], got_o[0]),
            jnp.where(first, got_o[0], keep_o[0]),
            jnp.where(first, keep_o[1], got_o[1]),
            jnp.where(first, got_o[1], keep_o[1]),
        ],
        axis=1,
    )

    qkv = mm(src, weight, 1, 0).astype(BF16)
    g = mm(cot, weight_o, 1, 1).astype(BF16)
    halo_kv = mm(halo, weight[:, 512:], 1, 0).astype(BF16)
    bias = jnp.where(ring == 0, -jnp.inf, 0.0).astype(F32).reshape(1, 1)
    dq, att_t, dk_halo, dk, dv_halo, dv = attention(bias, qkv, halo_kv, g)

    grad = jnp.concatenate([dq, dk, dv], axis=1)
    grad_halo = jnp.concatenate([dk_halo, dv_halo], axis=1)

    ig = jnp.concatenate(
        [mm(grad, weight, 1, 1).astype(BF16), mm(grad_halo, weight[:, 512:], 1, 1).astype(BF16)], axis=0
    )
    ig_keep = lax.dynamic_slice_in_dim(ig, core * 512, 512, 1)
    ig_got = other_core(lax.dynamic_slice_in_dim(ig, (1 - core) * 512, 512, 1))
    ig_sum = ig_keep.astype(F32) + ig_got.astype(F32)
    returned = move(ig_sum[512:].astype(BF16), last_ring)
    ig_own = (ig_sum[:512] + returned.astype(F32)).astype(BF16).reshape(8, 64, 512)
    back = lax.all_to_all(ig_own, "seq", 0, 0, axis_index_groups=Z_GROUPS, tiled=True)
    back = back.reshape(2, 4, 64, 512)
    back_keep = lax.dynamic_index_in_dim(back, core, 0, keepdims=False)
    back_got = other_core(lax.dynamic_index_in_dim(back, 1 - core, 0, keepdims=False))
    input_grad = jnp.concatenate(
        [jnp.where(first, back_keep, back_got), jnp.where(first, back_got, back_keep)], axis=-1
    )[None]

    wg = mm(src, grad, 0, 0)
    wg_halo = mm(halo, grad_halo, 0, 0)
    wg_qk = jnp.concatenate([wg[:, :512], wg[:, 512:1024] + wg_halo[:, :512]], axis=1).astype(BF16)
    wg_v = (wg[:, 1024:] + wg_halo[:, 512:]).astype(BF16)
    wg_o = mm(att_t, cot, 1, 0).astype(BF16)

    qk = spread_sum(wg_qk.reshape(4, 256, 1024), y, NY, along_y).astype(BF16)
    v = wg_v.reshape(8, 8, 16, 512).transpose(1, 0, 2, 3)
    v = spread_sum(v, z, NZ, along_z).astype(BF16)
    o = wg_o.reshape(2, 2, 128, 2, 512).transpose(3, 1, 0, 2, 4).reshape(4, 2, 128, 512)
    o = spread_sum(o, x, NX, along_x).astype(BF16)

    qk = qk.reshape(2, 8, 16, 1024).transpose(1, 0, 2, 3)
    qk = spread_sum(qk, z, NZ, along_z)
    v = spread_sum(v.reshape(4, 2, 16, 512), y, NY, along_y)
    o = o.reshape(2, 8, 16, 512).transpose(1, 0, 2, 3)
    o = spread_sum(o, z, NZ, along_z).astype(BF16)

    qkv_rows = jnp.concatenate([qk, v], axis=-1).astype(BF16)
    q_, k_, v_ = qkv_rows[..., :512], qkv_rows[..., 512:1024], qkv_rows[..., 1024:]
    pad = jnp.zeros_like(q_[..., :256])
    own0 = jnp.where(first, q_, jnp.concatenate([q_[..., :256], pad], axis=-1))
    own1 = jnp.where(first, k_, jnp.concatenate([q_[..., 256:], pad], axis=-1))
    own2 = jnp.where(first, jnp.concatenate([v_[..., :256], pad], axis=-1), k_)
    own3 = jnp.where(first, jnp.concatenate([v_[..., 256:], pad], axis=-1), v_)
    owners = jnp.stack([own0, own1, own2, own3], axis=1).reshape(8, 16, 512)
    x_groups = [
        [flat(yy, (r // 2) * 2 + xl, zz, r % 2) for xl in range(2) for r in range(4)]
        for yy in range(NY)
        for zz in range(NZ)
    ]
    arrived = lax.all_to_all(owners, BOTH, 0, 0, axis_index_groups=x_groups, tiled=True)
    arrived = jnp.sum(arrived.reshape(4, 2, 16, 512).astype(F32), axis=0)
    from0, from1 = arrived[0], arrived[1]
    qkv_grad = jnp.where(
        (rep == 0)[None, None],
        jnp.concatenate([from0, from1[:, :256]], axis=1),
        jnp.where(
            (rep == 1)[None, None],
            jnp.concatenate([from1[:, :256], from0], axis=1),
            jnp.where(
                (rep == 2)[None, None],
                jnp.concatenate([from1, from0[:, :256]], axis=1),
                jnp.concatenate([from0[:, :256], from1], axis=1),
            ),
        ),
    )

    pieces = o.reshape(2, 16, 2, 256).transpose(0, 2, 1, 3).reshape(4, 16, 256)
    empty = jnp.zeros_like(pieces)
    pieces = jnp.concatenate([jnp.where(first, pieces, empty), jnp.where(first, empty, pieces)], axis=0)
    y_groups = [
        [flat(yy, xx, zz, cc) for yy in range(NY) for cc in range(2)] for xx in range(NX) for zz in range(NZ)
    ]
    got = lax.all_to_all(pieces, BOTH, 0, 0, axis_index_groups=y_groups, tiled=True)
    out_grad = jnp.sum(got.astype(F32), axis=0)
    return (input_grad, qkv_grad, out_grad)


def solution(mesh):
    return jax.shard_map(
        body,
        mesh=mesh,
        in_specs=(
            P("rep", None, "seq", None),
            P("rep", None, "seq", None),
            P(None, "rep"),
            P(None, "rep"),
        ),
        out_specs=(P("rep", None, "seq", None), P("seq", "rep"), P("seq", "rep")),
        check_vma=False,
    )
```

```python
import jax
import jax.numpy as jnp
from jax import lax
from jax.experimental import pallas as pl
from jax.experimental.pallas import tpu as pltpu
from jax.sharding import PartitionSpec as P

D = 1024
HEADS = 16
HD = 64
WINDOW = 512
NY, NX, NZ = 4, 4, 8
BOTH = ("seq", "rep")
BF16 = jnp.bfloat16
F32 = jnp.float32
LOG2E = 1.4426950408889634
PARAMS = pltpu.CompilerParams(vmem_limit_bytes=48 * 1024 * 1024)


def flat(y, x, z, c):
    y, x, z = y % NY, x % NX, z % NZ
    return ((y * 2 + x % 2) * NZ + z) * 4 + (x // 2) * 2 + c


PLACES = [(y, x, z, c) for y in range(NY) for x in range(NX) for z in range(NZ) for c in range(2)]


def move(value, target):
    pairs = []
    for place in PLACES:
        goal = target(*place)
        if goal is not None:
            pairs.append((flat(*place), flat(*goal)))
    return lax.ppermute(value, BOTH, pairs)


def other_core(value):
    return move(value, lambda y, x, z, c: (y, x, z, 1 - c))


def mm(a, b, ca, cb):
    return lax.dot_general(a, b, (((ca,), (cb,)), ((), ())), preferred_element_type=F32)


def attention_kernel(bias_ref, q_ref, g_ref, k_ref, v_ref, dq_ref, att_ref, dk_ref, dv_ref):
    size = 256
    bias = bias_ref[0, 0]
    low = lax.broadcasted_iota(jnp.int32, (1, 2 * HD), 1) < HD
    upper = (
        lax.broadcasted_iota(jnp.int32, (size, size), 0) > lax.broadcasted_iota(jnp.int32, (size, size), 1)
    )
    factor = LOG2E * HD ** -0.5
    tiles = [slice(i * size, (i + 1) * size) for i in range(4)]
    keys = [k_ref[tile, :] for tile in tiles]
    vals = [v_ref[tile, :] for tile in tiles]
    keys_t = [k.T for k in keys]
    vals_t = [v.T for v in vals]
    dk = [None] * 4
    dv = [None] * 4

    def add(total, index, term):
        total[index] = term if total[index] is None else total[index] + term

    for block in range(2):
        rows = tiles[block]
        q_pair = q_ref[rows, :]
        g_pair = g_ref[rows, :]
        g_t = g_pair.T.astype(F32)
        dq_t = []
        for head in range(2):
            mine = low if head == 0 else jnp.logical_not(low)
            lanes = slice(head * HD, (head + 1) * HD)
            q = jnp.where(mine, q_pair, jnp.zeros_like(q_pair))
            g = jnp.where(mine, g_pair, jnp.zeros_like(g_pair))
            s0, s1, s2 = [mm(keys[block + i], q, 1, 1) for i in range(3)]
            edge = jnp.where(upper, s0 + bias, s2)
            if block == 0:
                s1 = s1 + bias
            top = jnp.maximum(
                jnp.max(edge, axis=0, keepdims=True), jnp.max(s1, axis=0, keepdims=True)
            )
            edge = jnp.exp2((edge - top) * factor)
            full = jnp.exp2((s1 - top) * factor)
            scale = 1.0 / (jnp.sum(edge, axis=0, keepdims=True) + jnp.sum(full, axis=0, keepdims=True))
            edge = edge * scale
            full = full * scale
            p0 = jnp.where(upper, edge, 0.0).astype(BF16)
            p1 = full.astype(BF16)
            p2 = jnp.where(upper, 0.0, edge).astype(BF16)
            att = (
                mm(vals_t[block][lanes], p0, 1, 0)
                + mm(vals_t[block + 1][lanes], p1, 1, 0)
                + mm(vals_t[block + 2][lanes], p2, 1, 0)
            )
            delta = jnp.sum(g_t[lanes] * att, axis=0, keepdims=True)
            att_ref[lanes, rows] = att.astype(BF16)
            d0, d1, d2 = [mm(vals[block + i], g, 1, 1) for i in range(3)]
            d_edge = edge * (jnp.where(upper, d0, d2) - delta)
            z0 = jnp.where(upper, d_edge, 0.0).astype(BF16)
            z1 = (full * (d1 - delta)).astype(BF16)
            z2 = jnp.where(upper, 0.0, d_edge).astype(BF16)
            dq_t.append(
                mm(keys_t[block][lanes], z0, 1, 0)
                + mm(keys_t[block + 1][lanes], z1, 1, 0)
                + mm(keys_t[block + 2][lanes], z2, 1, 0)
            )
            for i, (p, z) in enumerate(((p0, z0), (p1, z1), (p2, z2))):
                add(dv, block + i, mm(p, g, 1, 0))
                add(dk, block + i, mm(z, q, 1, 0))
        dq = jnp.concatenate(dq_t, axis=0) * (HD ** -0.5)
        dq_ref[rows, :] = dq.T.astype(BF16)
    for i, tile in enumerate(tiles):
        dk_ref[tile, :] = (dk[i] * (HD ** -0.5)).astype(BF16)
        dv_ref[tile, :] = dv[i].astype(BF16)


def attention(bias, qkv, g):
    tokens, width = g.shape
    pairs = width // (2 * HD)
    own = pl.BlockSpec((tokens, 2 * HD), lambda i: (0, i))
    long = pl.BlockSpec((2 * tokens, 2 * HD), lambda i: (0, i))
    return pl.pallas_call(
        attention_kernel,
        grid=(pairs,),
        in_specs=[
            pl.BlockSpec(memory_space=pltpu.SMEM),
            pl.BlockSpec((tokens, 2 * HD), lambda i: (1, i)),
            own,
            pl.BlockSpec((2 * tokens, 2 * HD), lambda i: (0, pairs + i)),
            pl.BlockSpec((2 * tokens, 2 * HD), lambda i: (0, 2 * pairs + i)),
        ],
        out_specs=[own, pl.BlockSpec((2 * HD, tokens), lambda i: (i, 0)), long, long],
        out_shape=[
            jax.ShapeDtypeStruct((tokens, width), BF16),
            jax.ShapeDtypeStruct((width, tokens), BF16),
            jax.ShapeDtypeStruct((2 * tokens, width), BF16),
            jax.ShapeDtypeStruct((2 * tokens, width), BF16),
        ],
        compiler_params=PARAMS,
        cost_estimate=pl.CostEstimate(
            flops=16 * 768 * 256 * 64 * 12, bytes_accessed=6 * 1024 * 1024, transcendentals=16 * 512 * 256
        ),
    )(bias, qkv, g, qkv, qkv)


def token_grad_kernel(*refs):
    out_ref = refs[-1]
    pairs = [(refs[2 * i], refs[2 * i + 1]) for i in range(len(refs) // 2)]
    for half in range(2):
        cols = slice(half * 512, (half + 1) * 512)
        acc = None
        for grad_ref, weight_ref in pairs:
            term = mm(grad_ref[...], weight_ref[cols, :], 1, 1)
            acc = term if acc is None else acc + term
        out_ref[half] = acc.astype(BF16)


def token_grad(rows, weight, dq, dk, dv):
    whole = pl.BlockSpec((512, 512), lambda i: (0, 0))
    tokens = pl.BlockSpec((512, 512), lambda i: (rows, 0))

    def cols(which):
        return pl.BlockSpec((1024, 512), lambda i: (0, which))

    specs, args = [], []
    if dq is not None:
        specs, args = [whole, cols(0)], [dq, weight]
    return pl.pallas_call(
        token_grad_kernel,
        grid=(1,),
        in_specs=specs + [tokens, cols(1), tokens, cols(2)],
        out_specs=pl.BlockSpec((2, 512, 512), lambda i: (0, 0, 0)),
        out_shape=jax.ShapeDtypeStruct((2, 512, 512), BF16),
        compiler_params=PARAMS,
        cost_estimate=pl.CostEstimate(
            flops=2 * 512 * 1024 * 512 * (len(args) // 2 + 2), bytes_accessed=5 << 20, transcendentals=0
        ),
    )(*args, dk, weight, dv, weight)


def weight_grad_a_kernel(src_ref, dq_ref, dk_ref, dv_ref, out_ref):
    for y in range(4):
        rows = slice(y * 256, (y + 1) * 256)
        out_ref[y, :, :256] = mm(src_ref[rows, 512:], dq_ref[...], 1, 0).astype(BF16)
        out_ref[y, :, 256:768] = mm(src_ref[rows, :], dk_ref[...], 1, 0).astype(BF16)
        out_ref[y, :, 768:] = mm(src_ref[rows, :], dv_ref[...], 1, 0).astype(BF16)


def weight_grad_c_kernel(src_ref, dq_ref, dv_ref, att_ref, cot_ref, out_ref):
    for y in range(4):
        rows = slice(y * 256, (y + 1) * 256)
        parts = (mm(src_ref[rows, 512:], dq_ref[...], 1, 0), mm(src_ref[rows, :], dv_ref[...], 1, 0))
        for hi in range(2):
            for lo in range(2):
                piece = parts[hi][lo * 128:(lo + 1) * 128].astype(BF16)
                out_ref[2 * hi + lo, y * 128:(y + 1) * 128, :] = piece
    for group in range(2):
        for rep in range(4):
            part = mm(att_ref[group * 256:(group + 1) * 256, :], cot_ref[:, rep * 256:(rep + 1) * 256], 1, 0)
            start = 512 + (2 * (rep % 2) + group) * 128
            for lo in range(2):
                piece = part[lo * 128:(lo + 1) * 128].astype(BF16)
                out_ref[2 * (rep // 2) + lo, start:start + 128, :] = piece


def weight_grads_a(src_t, dq, dk, dv):
    return pl.pallas_call(
        weight_grad_a_kernel,
        grid=(1,),
        in_specs=[
            pl.BlockSpec((1024, 1024), lambda i: (0, 0)),
            pl.BlockSpec((512, 256), lambda i: (0, 0)),
            pl.BlockSpec((1024, 512), lambda i: (0, 0)),
            pl.BlockSpec((1024, 256), lambda i: (0, 1)),
        ],
        out_specs=pl.BlockSpec((4, 256, 1024), lambda i: (0, 0, 0)),
        out_shape=jax.ShapeDtypeStruct((4, 256, 1024), BF16),
        compiler_params=PARAMS,
        cost_estimate=pl.CostEstimate(flops=2 * 1024 * 1024 * 900, bytes_accessed=6 << 20, transcendentals=0),
    )(src_t, dq, dk, dv)


def weight_grads_c(src_t, dq, dv, att_t, cot):
    return pl.pallas_call(
        weight_grad_c_kernel,
        grid=(1,),
        in_specs=[
            pl.BlockSpec((1024, 1024), lambda i: (0, 0)),
            pl.BlockSpec((512, 256), lambda i: (0, 1)),
            pl.BlockSpec((1024, 256), lambda i: (0, 0)),
            pl.BlockSpec((512, 512), lambda i: (0, 0)),
            pl.BlockSpec((512, 1024), lambda i: (0, 0)),
        ],
        out_specs=pl.BlockSpec((4, 1024, 256), lambda i: (0, 0, 0)),
        out_shape=jax.ShapeDtypeStruct((4, 1024, 256), BF16),
        compiler_params=PARAMS,
        cost_estimate=pl.CostEstimate(flops=2 * 1024 * 1024 * 640, bytes_accessed=6 << 20, transcendentals=0),
    )(src_t, dq, dv, att_t, cot)


def regroup(value, names, groups):
    return lax.all_to_all(value, names, 0, 0, axis_index_groups=groups, tiled=True)


def total(value, parts):
    return jnp.sum(value.reshape((parts,) + (-1,) + value.shape[1:]).astype(F32), axis=0)


def spread_sum(value, here, target):
    came = []
    for step in (1, 3, 2):
        chunk = lax.dynamic_index_in_dim(value, lax.rem(here + step, 4), 0, keepdims=False)
        came.append(move(chunk, lambda y, x, z, c, step=step: target(step, y, x, z, c)))
    mine = lax.dynamic_index_in_dim(value, here, 0, keepdims=False)
    return mine.astype(F32) + came[0].astype(F32) + came[1].astype(F32) + came[2].astype(F32)


def along_y(step, y, x, z, c):
    return (y + step, x, z, c)


def along_x(step, y, x, z, c):
    return (y, x + step, z, c)


ALL_Y, ALL_X, ALL_Z, ALL_C = range(NY), range(NX), range(NZ), range(2)
Z_GROUPS = [[ring * NZ + z for z in ALL_Z] for ring in range(8)]
Y_GROUPS = [[(y * 2 + xl) * NZ + z for y in ALL_Y] for xl in range(2) for z in ALL_Z]
XC_GROUPS = [
    [flat(y, 2 * xh + xl, z, c) for xl in range(2) for xh in range(2) for c in ALL_C] for y in ALL_Y for z in ALL_Z
]


def next_ring(y, x, z, c):
    ring = 2 * y + x % 2 + 1
    return None if ring == 8 else (ring // 2, (x // 2) * 2 + ring % 2, z, c)


def last_ring(y, x, z, c):
    ring = 2 * y + x % 2 - 1
    return None if ring < 0 else (ring // 2, (x // 2) * 2 + ring % 2, z, c)


def body(inputs, upstream, qkv_weight, out_weight):
    at = lax.axis_index("seq")
    rep = lax.axis_index("rep")
    core = lax.rem(rep, 2)
    ring = at // NZ
    y = ring // 2
    x = 2 * (rep // 2) + lax.rem(ring, 2)
    first = core == 0
    left = rep // 2 == 0

    def in_order(mine, other, axis):
        return jnp.concatenate([jnp.where(first, mine, other), jnp.where(first, other, mine)], axis=axis)

    def groups_of(out, core):
        out = out.reshape(4, 256, 256)
        return jnp.concatenate(
            [lax.dynamic_index_in_dim(out, core, 0, False), lax.dynamic_index_in_dim(out, 2 + core, 0, False)],
            axis=0,
        )

    def across(y, x, z, c):
        return (y, 3 - x, z, c)

    near_give = jnp.concatenate([qkv_weight[:, 256:512], groups_of(out_weight, 1 - core)], axis=0)
    near = jnp.concatenate(
        [qkv_weight[:, :256], qkv_weight[:, 512:], groups_of(out_weight, core)], axis=0
    )
    far_give = move(near_give, across)
    far = move(near, across)
    near_swap = other_core(near_give)
    far_swap = other_core(far_give)

    def to_chips(tokens):
        low, high = tokens[..., :512], tokens[..., 512:]
        other = other_core(jnp.where(first, high, low))
        mixed = in_order(jnp.where(first, low, high), other, 0)
        return regroup(mixed, "seq", Z_GROUPS).reshape(NZ * 64, 512)

    src = to_chips(inputs[0])
    halo = move(src, next_ring)
    cot = to_chips(upstream[0])
    src = jnp.concatenate([halo, src], axis=0)
    src = in_order(src, other_core(src), 1)
    cot = in_order(cot, other_core(cot), 1)

    lo, hi = jnp.where(left, near, far), jnp.where(left, far, near)
    lo_swap, hi_swap = jnp.where(left, near_swap, far_swap), jnp.where(left, far_swap, near_swap)
    weight = jnp.concatenate(
        [
            jnp.where(first, lo[:1024], lo_swap[:1024]),
            jnp.where(first, lo[1024:2048], lo[:1024]),
            jnp.where(first, lo_swap[:1024], lo[1024:2048]),
            jnp.where(first, hi[:1024], hi_swap[:1024]),
            jnp.where(first, hi[1024:2048], hi[:1024]),
            jnp.where(first, hi_swap[:1024], hi[1024:2048]),
        ],
        axis=1,
    )
    weight_o = jnp.concatenate(
        [in_order(lo[2048:], lo_swap[1024:], 1), in_order(hi[2048:], hi_swap[1024:], 1)], axis=1
    )
    src_t = src.T

    qkv = mm(src, weight, 1, 0).astype(BF16)
    g = mm(cot, weight_o, 1, 1).astype(BF16)
    bias = jnp.where(ring == 0, -jnp.inf, 0.0).astype(F32).reshape(1, 1)
    dq, att_t, dk, dv = attention(bias, qkv, g)

    def core_sum(value):
        mine = lax.dynamic_index_in_dim(value, core, 0, keepdims=False)
        other = other_core(lax.dynamic_index_in_dim(value, 1 - core, 0, keepdims=False))
        return mine.astype(F32) + other.astype(F32)

    ig_halo = token_grad(0, weight, None, dk, dv)
    returned = move(core_sum(ig_halo).astype(BF16), last_ring)
    dq, dk, dv, ig_halo = lax.optimization_barrier((dq, dk, dv, ig_halo))

    part_a = weight_grads_a(src_t, dq, dk, dv)
    dq, dk, dv, part_a = lax.optimization_barrier((dq, dk, dv, part_a))
    part_a = total(regroup(part_a, "seq", Y_GROUPS), NY)[0].astype(BF16)

    part_c = weight_grads_c(src_t, dq, dv, att_t, cot)
    dq, dk, dv, part_c = lax.optimization_barrier((dq, dk, dv, part_c))
    part_c = spread_sum(part_c, x, along_x).astype(BF16)

    ig = core_sum(token_grad(1, weight, dq, dk, dv))
    ig = (ig + returned.astype(F32)).astype(BF16).reshape(8, 64, 512)
    ig = regroup(ig, "seq", Z_GROUPS).reshape(2, 4, 64, 512)
    kept = lax.dynamic_index_in_dim(ig, core, 0, keepdims=False)
    came = other_core(lax.dynamic_index_in_dim(ig, 1 - core, 0, keepdims=False))
    input_grad = in_order(kept, came, -1)[None]

    part_a = part_a.reshape(2, 128, 4, 256).transpose(0, 2, 1, 3).reshape(8, 128, 256)
    part_a = regroup(part_a, BOTH, XC_GROUPS).reshape(4, 2, 128, 256)
    part_a = jnp.sum(part_a.astype(F32), axis=0).astype(BF16)

    part_o = part_c[512:].reshape(2, 2, 1, 128, 256)
    mine = lax.dynamic_index_in_dim(part_o, core, 0, keepdims=False)
    other = other_core(lax.dynamic_index_in_dim(part_o, 1 - core, 0, keepdims=False))
    part_o = in_order(mine, other, 1).reshape(4, 128, 256)
    part_c = jnp.concatenate([part_c[:512].reshape(4, 128, 256), part_o], axis=1)
    part_c = spread_sum(part_c, y, along_y).astype(BF16).reshape(2, 128, 256)

    last = jnp.concatenate([part_a, part_c], axis=0).reshape(4, 8, 16, 256).transpose(1, 0, 2, 3)
    last = jnp.sum(regroup(last, "seq", Z_GROUPS).astype(F32), axis=0)
    qkv_grad = jnp.where(
        first,
        jnp.concatenate([last[0], last[1], last[2]], axis=1),
        jnp.concatenate([last[2], last[0], last[1]], axis=1),
    )
    return input_grad, qkv_grad, last[3]


def solution(mesh):
    return jax.shard_map(
        body,
        mesh=mesh,
        in_specs=(
            P("rep", None, "seq", None),
            P("rep", None, "seq", None),
            P(None, "rep"),
            P(None, "rep"),
        ),
        out_specs=(P("rep", None, "seq", None), P("seq", "rep"), P("seq", "rep")),
        check_vma=False,
    )
```

```python
import jax
import jax.numpy as jnp
from jax import lax
from jax.experimental import pallas as pl
from jax.experimental.pallas import tpu as pltpu
from jax.sharding import PartitionSpec as P

D = 1024
HEADS = 16
HD = 64
WINDOW = 512
NY, NX, NZ = 4, 4, 8
BOTH = ("seq", "rep")
BF16 = jnp.bfloat16
F32 = jnp.float32
LOG2E = 1.4426950408889634
PARAMS = pltpu.CompilerParams(vmem_limit_bytes=48 * 1024 * 1024)


def flat(y, x, z, c):
    y, x, z = y % NY, x % NX, z % NZ
    return ((y * 2 + x % 2) * NZ + z) * 4 + (x // 2) * 2 + c


PLACES = [(y, x, z, c) for y in range(NY) for x in range(NX) for z in range(NZ) for c in range(2)]


def move(value, target):
    pairs = []
    for place in PLACES:
        goal = target(*place)
        if goal is not None:
            pairs.append((flat(*place), flat(*goal)))
    return lax.ppermute(value, BOTH, pairs)


def other_core(value):
    return move(value, lambda y, x, z, c: (y, x, z, 1 - c))


def mm(a, b, ca, cb):
    return lax.dot_general(a, b, (((ca,), (cb,)), ((), ())), preferred_element_type=F32)


def attention_kernel(bias_ref, q_ref, g_ref, k_ref, v_ref, dq_ref, att_ref, dk_ref, dv_ref):
    size = 256
    bias = bias_ref[0, 0]
    low = lax.broadcasted_iota(jnp.int32, (1, 2 * HD), 1) < HD
    upper = (
        lax.broadcasted_iota(jnp.int32, (size, size), 0) > lax.broadcasted_iota(jnp.int32, (size, size), 1)
    )
    factor = LOG2E * HD ** -0.5
    tiles = [slice(i * size, (i + 1) * size) for i in range(4)]
    keys = [k_ref[tile, :] for tile in tiles]
    vals = [v_ref[tile, :] for tile in tiles]
    keys_t = [k.T for k in keys]
    vals_t = [v.T for v in vals]
    dk = [None] * 4
    dv = [None] * 4

    def add(total, index, term):
        total[index] = term if total[index] is None else total[index] + term

    for block in range(2):
        rows = tiles[block]
        q_pair = q_ref[rows, :]
        g_pair = g_ref[rows, :]
        g_t = g_pair.T.astype(F32)
        dq_t = []
        for head in range(2):
            mine = low if head == 0 else jnp.logical_not(low)
            lanes = slice(head * HD, (head + 1) * HD)
            q = jnp.where(mine, q_pair, jnp.zeros_like(q_pair))
            g = jnp.where(mine, g_pair, jnp.zeros_like(g_pair))
            s0, s1, s2 = [mm(keys[block + i], q, 1, 1) for i in range(3)]
            edge = jnp.where(upper, s0 + bias, s2)
            if block == 0:
                s1 = s1 + bias
            top = jnp.maximum(
                jnp.max(edge, axis=0, keepdims=True), jnp.max(s1, axis=0, keepdims=True)
            )
            edge = jnp.exp2((edge - top) * factor)
            full = jnp.exp2((s1 - top) * factor)
            scale = 1.0 / (jnp.sum(edge, axis=0, keepdims=True) + jnp.sum(full, axis=0, keepdims=True))
            edge = edge * scale
            full = full * scale
            p0 = jnp.where(upper, edge, 0.0).astype(BF16)
            p1 = full.astype(BF16)
            p2 = jnp.where(upper, 0.0, edge).astype(BF16)
            att = (
                mm(vals_t[block][lanes], p0, 1, 0)
                + mm(vals_t[block + 1][lanes], p1, 1, 0)
                + mm(vals_t[block + 2][lanes], p2, 1, 0)
            )
            delta = jnp.sum(g_t[lanes] * att, axis=0, keepdims=True)
            att_ref[lanes, rows] = att.astype(BF16)
            d0, d1, d2 = [mm(vals[block + i], g, 1, 1) for i in range(3)]
            d_edge = edge * (jnp.where(upper, d0, d2) - delta)
            z0 = jnp.where(upper, d_edge, 0.0).astype(BF16)
            z1 = (full * (d1 - delta)).astype(BF16)
            z2 = jnp.where(upper, 0.0, d_edge).astype(BF16)
            dq_t.append(
                mm(keys_t[block][lanes], z0, 1, 0)
                + mm(keys_t[block + 1][lanes], z1, 1, 0)
                + mm(keys_t[block + 2][lanes], z2, 1, 0)
            )
            for i, (p, z) in enumerate(((p0, z0), (p1, z1), (p2, z2))):
                add(dv, block + i, mm(p, g, 1, 0))
                add(dk, block + i, mm(z, q, 1, 0))
        dq = jnp.concatenate(dq_t, axis=0) * (HD ** -0.5)
        dq_ref[rows, :] = dq.T.astype(BF16)
    for i, tile in enumerate(tiles):
        dk_ref[tile, :] = (dk[i] * (HD ** -0.5)).astype(BF16)
        dv_ref[tile, :] = dv[i].astype(BF16)


def attention(bias, qkv, g):
    tokens, width = g.shape
    pairs = width // (2 * HD)
    own = pl.BlockSpec((tokens, 2 * HD), lambda i: (0, i))
    long = pl.BlockSpec((2 * tokens, 2 * HD), lambda i: (0, i))
    return pl.pallas_call(
        attention_kernel,
        grid=(pairs,),
        in_specs=[
            pl.BlockSpec(memory_space=pltpu.SMEM),
            pl.BlockSpec((tokens, 2 * HD), lambda i: (1, i)),
            own,
            pl.BlockSpec((2 * tokens, 2 * HD), lambda i: (0, pairs + i)),
            pl.BlockSpec((2 * tokens, 2 * HD), lambda i: (0, 2 * pairs + i)),
        ],
        out_specs=[own, pl.BlockSpec((2 * HD, tokens), lambda i: (i, 0)), long, long],
        out_shape=[
            jax.ShapeDtypeStruct((tokens, width), BF16),
            jax.ShapeDtypeStruct((width, tokens), BF16),
            jax.ShapeDtypeStruct((2 * tokens, width), BF16),
            jax.ShapeDtypeStruct((2 * tokens, width), BF16),
        ],
        compiler_params=PARAMS,
        cost_estimate=pl.CostEstimate(
            flops=16 * 768 * 256 * 64 * 12, bytes_accessed=6 * 1024 * 1024, transcendentals=16 * 512 * 256
        ),
    )(bias, qkv, g, qkv, qkv)


def token_grad_kernel(*refs):
    out_ref = refs[-1]
    pairs = [(refs[2 * i], refs[2 * i + 1]) for i in range(len(refs) // 2)]
    for half in range(2):
        cols = slice(half * 512, (half + 1) * 512)
        acc = None
        for grad_ref, weight_ref in pairs:
            term = mm(grad_ref[...], weight_ref[cols, :], 1, 1)
            acc = term if acc is None else acc + term
        out_ref[half] = acc.astype(BF16)


def token_grad(rows, weight, dq, dk, dv):
    whole = pl.BlockSpec((512, 512), lambda i: (0, 0))
    tokens = pl.BlockSpec((512, 512), lambda i: (rows, 0))

    def cols(which):
        return pl.BlockSpec((1024, 512), lambda i: (0, which))

    specs, args = [], []
    if dq is not None:
        specs, args = [whole, cols(0)], [dq, weight]
    return pl.pallas_call(
        token_grad_kernel,
        grid=(1,),
        in_specs=specs + [tokens, cols(1), tokens, cols(2)],
        out_specs=pl.BlockSpec((2, 512, 512), lambda i: (0, 0, 0)),
        out_shape=jax.ShapeDtypeStruct((2, 512, 512), BF16),
        compiler_params=PARAMS,
        cost_estimate=pl.CostEstimate(
            flops=2 * 512 * 1024 * 512 * (len(args) // 2 + 2), bytes_accessed=5 << 20, transcendentals=0
        ),
    )(*args, dk, weight, dv, weight)


def weight_grad_a_kernel(src_ref, dq_ref, dk_ref, dv_ref, out_ref):
    for y in range(4):
        rows = slice(y * 256, (y + 1) * 256)
        out_ref[y, :, :256] = mm(src_ref[rows, 512:], dq_ref[...], 1, 0).astype(BF16)
        out_ref[y, :, 256:768] = mm(src_ref[rows, :], dk_ref[...], 1, 0).astype(BF16)
        out_ref[y, :, 768:] = mm(src_ref[rows, :], dv_ref[...], 1, 0).astype(BF16)


def weight_grad_c_kernel(src_ref, dq_ref, dv_ref, att_ref, cot_ref, out_ref):
    for y in range(4):
        rows = slice(y * 256, (y + 1) * 256)
        parts = (mm(src_ref[rows, 512:], dq_ref[...], 1, 0), mm(src_ref[rows, :], dv_ref[...], 1, 0))
        for hi in range(2):
            for lo in range(2):
                piece = parts[hi][lo * 128:(lo + 1) * 128].astype(BF16)
                out_ref[2 * hi + lo, y * 128:(y + 1) * 128, :] = piece
    for group in range(2):
        for rep in range(4):
            part = mm(att_ref[group * 256:(group + 1) * 256, :], cot_ref[:, rep * 256:(rep + 1) * 256], 1, 0)
            start = 512 + (2 * (rep % 2) + group) * 128
            for lo in range(2):
                piece = part[lo * 128:(lo + 1) * 128].astype(BF16)
                out_ref[2 * (rep // 2) + lo, start:start + 128, :] = piece


def weight_grads_a(src_t, dq, dk, dv):
    return pl.pallas_call(
        weight_grad_a_kernel,
        grid=(1,),
        in_specs=[
            pl.BlockSpec((1024, 1024), lambda i: (0, 0)),
            pl.BlockSpec((512, 256), lambda i: (0, 0)),
            pl.BlockSpec((1024, 512), lambda i: (0, 0)),
            pl.BlockSpec((1024, 256), lambda i: (0, 1)),
        ],
        out_specs=pl.BlockSpec((4, 256, 1024), lambda i: (0, 0, 0)),
        out_shape=jax.ShapeDtypeStruct((4, 256, 1024), BF16),
        compiler_params=PARAMS,
        cost_estimate=pl.CostEstimate(flops=2 * 1024 * 1024 * 900, bytes_accessed=6 << 20, transcendentals=0),
    )(src_t, dq, dk, dv)


def weight_grads_c(src_t, dq, dv, att_t, cot):
    return pl.pallas_call(
        weight_grad_c_kernel,
        grid=(1,),
        in_specs=[
            pl.BlockSpec((1024, 1024), lambda i: (0, 0)),
            pl.BlockSpec((512, 256), lambda i: (0, 1)),
            pl.BlockSpec((1024, 256), lambda i: (0, 0)),
            pl.BlockSpec((512, 512), lambda i: (0, 0)),
            pl.BlockSpec((512, 1024), lambda i: (0, 0)),
        ],
        out_specs=pl.BlockSpec((4, 1024, 256), lambda i: (0, 0, 0)),
        out_shape=jax.ShapeDtypeStruct((4, 1024, 256), BF16),
        compiler_params=PARAMS,
        cost_estimate=pl.CostEstimate(flops=2 * 1024 * 1024 * 640, bytes_accessed=6 << 20, transcendentals=0),
    )(src_t, dq, dv, att_t, cot)


def regroup(value, names, groups):
    return lax.all_to_all(value, names, 0, 0, axis_index_groups=groups, tiled=True)


def after(value, *events):
    return lax.optimization_barrier((value,) + events)[0]


def chunks(value, here):
    return [
        lax.dynamic_index_in_dim(value, lax.rem(here + step, 4), 0, keepdims=False) for step in (0, 1, 3, 2)
    ]


def spread_sum(pieces, target, *events):
    out = pieces[0].astype(F32)
    came = [
        move(piece, lambda y, x, z, c, step=step: target(step, y, x, z, c))
        for step, piece in zip((1, 3, 2), pieces[1:])
    ]
    for piece in came:
        out = out + after(piece, *events).astype(F32)
    return out.astype(BF16)


def along_y(step, y, x, z, c):
    return (y + step, x, z, c)


def along_x(step, y, x, z, c):
    return (y, x + step, z, c)


ALL_Y, ALL_X, ALL_Z, ALL_C = range(NY), range(NX), range(NZ), range(2)
Z_GROUPS = [[ring * NZ + z for z in ALL_Z] for ring in range(8)]
XC_GROUPS = [
    [flat(y, 2 * xh + xl, z, c) for xl in range(2) for xh in range(2) for c in ALL_C] for y in ALL_Y for z in ALL_Z
]


def next_ring(y, x, z, c):
    ring = 2 * y + x % 2 + 1
    return None if ring == 8 else (ring // 2, (x // 2) * 2 + ring % 2, z, c)


def last_ring(y, x, z, c):
    ring = 2 * y + x % 2 - 1
    return None if ring < 0 else (ring // 2, (x // 2) * 2 + ring % 2, z, c)


def body(inputs, upstream, qkv_weight, out_weight):
    at = lax.axis_index("seq")
    rep = lax.axis_index("rep")
    core = lax.rem(rep, 2)
    ring = at // NZ
    y = ring // 2
    x = 2 * (rep // 2) + lax.rem(ring, 2)
    first = core == 0
    left = rep // 2 == 0

    def in_order(mine, other, axis):
        return jnp.concatenate([jnp.where(first, mine, other), jnp.where(first, other, mine)], axis=axis)

    def groups_of(out, core):
        out = out.reshape(4, 256, 256)
        return jnp.concatenate(
            [lax.dynamic_index_in_dim(out, core, 0, False), lax.dynamic_index_in_dim(out, 2 + core, 0, False)],
            axis=0,
        )

    def across(y, x, z, c):
        return (y, 3 - x, z, c)

    cross = jnp.concatenate(
        [
            lax.dynamic_slice_in_dim(qkv_weight, y * 256, 256, 0),
            lax.dynamic_slice_in_dim(out_weight, y * 256, 256, 0),
        ],
        axis=1,
    )
    cross = move(cross, across)
    far_rows = jnp.zeros((1024, 1024), BF16)
    far_rows = lax.dynamic_update_slice_in_dim(far_rows, cross, y * 256, 0)
    for step in (1, 3, 2):
        piece = move(cross, lambda y, x, z, c, step=step: (y + step, x, z, c))
        far_rows = lax.dynamic_update_slice_in_dim(far_rows, piece, lax.rem(y + 4 - step, 4) * 256, 0)

    def to_give(qkv, out):
        return jnp.concatenate([qkv[:, 256:512], groups_of(out, 1 - core)], axis=0)

    def to_keep(qkv, out):
        return jnp.concatenate([qkv[:, :256], qkv[:, 512:768], groups_of(out, core)], axis=0)

    near = to_keep(qkv_weight, out_weight)
    far = to_keep(far_rows, far_rows[:, 768:])
    near_swap = other_core(to_give(qkv_weight, out_weight))
    far_swap = other_core(to_give(far_rows, far_rows[:, 768:]))

    def to_chips(tokens):
        low, high = tokens[..., :512], tokens[..., 512:]
        other = other_core(jnp.where(first, high, low))
        mixed = in_order(jnp.where(first, low, high), other, 0)
        return regroup(mixed, "seq", Z_GROUPS).reshape(NZ * 64, 512)

    src = to_chips(inputs[0])
    halo = move(src, next_ring)
    cot = to_chips(upstream[0])
    src = jnp.concatenate([halo, src], axis=0)
    src = in_order(src, other_core(src), 1)
    cot = in_order(cot, other_core(cot), 1)

    lo, hi = jnp.where(left, near, far), jnp.where(left, far, near)
    lo_swap, hi_swap = jnp.where(left, near_swap, far_swap), jnp.where(left, far_swap, near_swap)
    weight = jnp.concatenate(
        [
            jnp.where(first, lo[:1024], lo_swap[:1024]),
            jnp.where(first, lo[1024:2048], lo[:1024]),
            jnp.where(first, lo_swap[:1024], lo[1024:2048]),
            jnp.where(first, hi[:1024], hi_swap[:1024]),
            jnp.where(first, hi[1024:2048], hi[:1024]),
            jnp.where(first, hi_swap[:1024], hi[1024:2048]),
        ],
        axis=1,
    )
    weight_o = jnp.concatenate(
        [in_order(lo[2048:], lo_swap[1024:], 1), in_order(hi[2048:], hi_swap[1024:], 1)], axis=1
    )
    src_t = src.T

    qkv = mm(src, weight, 1, 0).astype(BF16)
    g = mm(cot, weight_o, 1, 1).astype(BF16)
    bias = jnp.where(ring == 0, -jnp.inf, 0.0).astype(F32).reshape(1, 1)
    dq, att_t, dk, dv = attention(bias, qkv, g)

    def core_sum(value):
        mine = lax.dynamic_index_in_dim(value, core, 0, keepdims=False)
        other = other_core(lax.dynamic_index_in_dim(value, 1 - core, 0, keepdims=False))
        return mine.astype(F32) + other.astype(F32)

    ig_halo = token_grad(0, weight, None, dk, dv)

    part_a = chunks(weight_grads_a(src_t, dq, after(dk, ig_halo), dv), y)
    ig_halo = core_sum(ig_halo).astype(BF16)
    returned = move(ig_halo, last_ring)

    part_c = chunks(weight_grads_c(src_t, after(dq, ig_halo, *part_a), dv, att_t, cot), x)
    ig = token_grad(1, weight, after(dq, *part_c), dk, dv)
    part_a = spread_sum(part_a, along_y, ig)
    part_c = spread_sum(part_c, along_x, ig)

    ig = (core_sum(ig) + returned.astype(F32)).astype(BF16).reshape(8, 64, 512)
    ig = regroup(ig, "seq", Z_GROUPS).reshape(2, 4, 64, 512)
    part_a = after(part_a, ig)
    kept = lax.dynamic_index_in_dim(ig, core, 0, keepdims=False)
    came = other_core(lax.dynamic_index_in_dim(ig, 1 - core, 0, keepdims=False))
    input_grad = in_order(kept, came, -1)[None]

    part_a = part_a.reshape(2, 128, 4, 256).transpose(0, 2, 1, 3).reshape(8, 128, 256)
    part_a = regroup(part_a, BOTH, XC_GROUPS).reshape(4, 2, 128, 256)
    part_a = jnp.sum(part_a.astype(F32), axis=0).astype(BF16)

    part_o = part_c[512:].reshape(2, 2, 1, 128, 256)
    mine = lax.dynamic_index_in_dim(part_o, core, 0, keepdims=False)
    other = other_core(lax.dynamic_index_in_dim(part_o, 1 - core, 0, keepdims=False))
    part_o = in_order(mine, other, 1).reshape(4, 128, 256)
    part_c = jnp.concatenate([part_c[:512].reshape(4, 128, 256), part_o], axis=1)
    part_c = spread_sum(chunks(part_c, y), along_y).reshape(2, 128, 256)

    last = jnp.concatenate([part_a, part_c], axis=0).reshape(4, 8, 16, 256).transpose(1, 0, 2, 3)
    last = jnp.sum(regroup(last, "seq", Z_GROUPS).astype(F32), axis=0)
    qkv_grad = jnp.where(
        first,
        jnp.concatenate([last[0], last[1], last[2]], axis=1),
        jnp.concatenate([last[2], last[0], last[1]], axis=1),
    )
    return input_grad, qkv_grad, last[3]


def solution(mesh):
    return jax.shard_map(
        body,
        mesh=mesh,
        in_specs=(
            P("rep", None, "seq", None),
            P("rep", None, "seq", None),
            P(None, "rep"),
            P(None, "rep"),
        ),
        out_specs=(P("rep", None, "seq", None), P("seq", "rep"), P("seq", "rep")),
        check_vma=False,
    )
```

```python
import jax
import jax.numpy as jnp
from jax import lax
from jax.experimental import pallas as pl
from jax.experimental.pallas import tpu as pltpu
from jax.sharding import PartitionSpec as P

D = 1024
HEADS = 16
HD = 64
WINDOW = 512
NY, NX, NZ = 4, 4, 8
BOTH = ("seq", "rep")
BF16 = jnp.bfloat16
F32 = jnp.float32
LOG2E = 1.4426950408889634
PARAMS = pltpu.CompilerParams(vmem_limit_bytes=48 * 1024 * 1024)


def flat(y, x, z, c):
    y, x, z = y % NY, x % NX, z % NZ
    return ((y * 2 + x % 2) * NZ + z) * 4 + (x // 2) * 2 + c


PLACES = [(y, x, z, c) for y in range(NY) for x in range(NX) for z in range(NZ) for c in range(2)]


def move(value, target):
    pairs = []
    for place in PLACES:
        goal = target(*place)
        if goal is not None:
            pairs.append((flat(*place), flat(*goal)))
    return lax.ppermute(value, BOTH, pairs)


def other_core(value):
    return move(value, lambda y, x, z, c: (y, x, z, 1 - c))


def mm(a, b, ca, cb):
    return lax.dot_general(a, b, (((ca,), (cb,)), ((), ())), preferred_element_type=F32)


def attention_kernel(bias_ref, q_ref, g_ref, k_ref, v_ref, dq_ref, att_ref, dk_ref, dv_ref):
    size = 256
    bias = bias_ref[0, 0]
    low = lax.broadcasted_iota(jnp.int32, (1, 2 * HD), 1) < HD
    upper = (
        lax.broadcasted_iota(jnp.int32, (size, size), 0) > lax.broadcasted_iota(jnp.int32, (size, size), 1)
    )
    upper_low = jnp.where(upper, 1.0, 0.0).astype(BF16)
    factor = LOG2E * HD ** -0.5
    tiles = [slice(i * size, (i + 1) * size) for i in range(4)]
    keys = [k_ref[tile, :] for tile in tiles]
    vals = [v_ref[tile, :] for tile in tiles]
    keys_t = [k.T for k in keys]
    vals_t = [v.T for v in vals]
    dk = [None] * 4
    dv = [None] * 4

    def add(total, index, term):
        total[index] = term if total[index] is None else total[index] + term

    for block in range(2):
        rows = tiles[block]
        q_pair = q_ref[rows, :]
        g_pair = g_ref[rows, :]
        g_t = g_pair.T.astype(F32)
        dq_t = []
        for head in range(2):
            mine = low if head == 0 else jnp.logical_not(low)
            lanes = slice(head * HD, (head + 1) * HD)
            q = jnp.where(mine, q_pair, jnp.zeros_like(q_pair))
            g = jnp.where(mine, g_pair, jnp.zeros_like(g_pair))
            s0, s1, s2 = [mm(keys[block + i], q, 1, 1) for i in range(3)]
            edge = jnp.where(upper, s0 + bias, s2)
            if block == 0:
                s1 = s1 + bias
            top = jnp.maximum(
                jnp.max(edge, axis=0, keepdims=True), jnp.max(s1, axis=0, keepdims=True)
            )
            edge = jnp.exp2((edge - top) * factor)
            full = jnp.exp2((s1 - top) * factor)
            scale = 1.0 / (jnp.sum(edge, axis=0, keepdims=True) + jnp.sum(full, axis=0, keepdims=True))
            edge = edge * scale
            full = full * scale
            edge_low = edge.astype(BF16)
            p0 = edge_low * upper_low
            p1 = full.astype(BF16)
            p2 = edge_low - p0
            att = (
                mm(vals_t[block][lanes], p0, 1, 0)
                + mm(vals_t[block + 1][lanes], p1, 1, 0)
                + mm(vals_t[block + 2][lanes], p2, 1, 0)
            )
            delta = jnp.sum(g_t[lanes] * att, axis=0, keepdims=True)
            att_ref[lanes, rows] = att.astype(BF16)
            d0, d1, d2 = [mm(vals[block + i], g, 1, 1) for i in range(3)]
            d_edge = (edge * (jnp.where(upper, d0, d2) - delta)).astype(BF16)
            z0 = d_edge * upper_low
            z1 = (full * (d1 - delta)).astype(BF16)
            z2 = d_edge - z0
            dq_t.append(
                mm(keys_t[block][lanes], z0, 1, 0)
                + mm(keys_t[block + 1][lanes], z1, 1, 0)
                + mm(keys_t[block + 2][lanes], z2, 1, 0)
            )
            for i, (p, z) in enumerate(((p0, z0), (p1, z1), (p2, z2))):
                add(dv, block + i, mm(p, g, 1, 0))
                add(dk, block + i, mm(z, q, 1, 0))
        dq = jnp.concatenate(dq_t, axis=0) * (HD ** -0.5)
        dq_ref[rows, :] = dq.T.astype(BF16)
    for i, tile in enumerate(tiles):
        dk_ref[tile, :] = (dk[i] * (HD ** -0.5)).astype(BF16)
        dv_ref[tile, :] = dv[i].astype(BF16)


def attention(bias, qkv, g):
    tokens, width = g.shape
    pairs = width // (2 * HD)
    own = pl.BlockSpec((tokens, 2 * HD), lambda i: (0, i))
    long = pl.BlockSpec((2 * tokens, 2 * HD), lambda i: (0, i))
    return pl.pallas_call(
        attention_kernel,
        grid=(pairs,),
        in_specs=[
            pl.BlockSpec(memory_space=pltpu.SMEM),
            pl.BlockSpec((tokens, 2 * HD), lambda i: (1, i)),
            own,
            pl.BlockSpec((2 * tokens, 2 * HD), lambda i: (0, pairs + i)),
            pl.BlockSpec((2 * tokens, 2 * HD), lambda i: (0, 2 * pairs + i)),
        ],
        out_specs=[own, pl.BlockSpec((2 * HD, tokens), lambda i: (i, 0)), long, long],
        out_shape=[
            jax.ShapeDtypeStruct((tokens, width), BF16),
            jax.ShapeDtypeStruct((width, tokens), BF16),
            jax.ShapeDtypeStruct((2 * tokens, width), BF16),
            jax.ShapeDtypeStruct((2 * tokens, width), BF16),
        ],
        compiler_params=PARAMS,
        cost_estimate=pl.CostEstimate(
            flops=16 * 768 * 256 * 64 * 12, bytes_accessed=6 * 1024 * 1024, transcendentals=16 * 512 * 256
        ),
    )(bias, qkv, g, qkv, qkv)


def token_grad_kernel(*refs):
    out_ref = refs[-1]
    pairs = [(refs[2 * i], refs[2 * i + 1]) for i in range(len(refs) // 2)]
    for half in range(2):
        cols = slice(half * 512, (half + 1) * 512)
        acc = None
        for grad_ref, weight_ref in pairs:
            term = mm(grad_ref[...], weight_ref[cols, :], 1, 1)
            acc = term if acc is None else acc + term
        out_ref[half] = acc.astype(BF16)


def token_grad(rows, weight, dq, dk, dv):
    whole = pl.BlockSpec((512, 512), lambda i: (0, 0))
    tokens = pl.BlockSpec((512, 512), lambda i: (rows, 0))

    def cols(which):
        return pl.BlockSpec((1024, 512), lambda i: (0, which))

    specs, args = [], []
    if dq is not None:
        specs, args = [whole, cols(0)], [dq, weight]
    return pl.pallas_call(
        token_grad_kernel,
        grid=(1,),
        in_specs=specs + [tokens, cols(1), tokens, cols(2)],
        out_specs=pl.BlockSpec((2, 512, 512), lambda i: (0, 0, 0)),
        out_shape=jax.ShapeDtypeStruct((2, 512, 512), BF16),
        compiler_params=PARAMS,
        cost_estimate=pl.CostEstimate(
            flops=2 * 512 * 1024 * 512 * (len(args) // 2 + 2), bytes_accessed=5 << 20, transcendentals=0
        ),
    )(*args, dk, weight, dv, weight)


def weight_grad_a_kernel(src_ref, dq_ref, dk_ref, dv_ref, out_ref):
    for y in range(4):
        rows = slice(y * 256, (y + 1) * 256)
        out_ref[y, :, :256] = mm(src_ref[rows, 512:], dq_ref[...], 1, 0).astype(BF16)
        out_ref[y, :, 256:768] = mm(src_ref[rows, :], dk_ref[...], 1, 0).astype(BF16)
        out_ref[y, :, 768:] = mm(src_ref[rows, :], dv_ref[...], 1, 0).astype(BF16)


def weight_grad_c_kernel(src_ref, dq_ref, dv_ref, att_ref, cot_ref, out_ref):
    for y in range(4):
        rows = slice(y * 256, (y + 1) * 256)
        parts = (mm(src_ref[rows, 512:], dq_ref[...], 1, 0), mm(src_ref[rows, :], dv_ref[...], 1, 0))
        for hi in range(2):
            for lo in range(2):
                piece = parts[hi][lo * 128:(lo + 1) * 128].astype(BF16)
                out_ref[2 * hi + lo, y * 128:(y + 1) * 128, :] = piece
    for group in range(2):
        for rep in range(4):
            part = mm(att_ref[group * 256:(group + 1) * 256, :], cot_ref[:, rep * 256:(rep + 1) * 256], 1, 0)
            start = 512 + (2 * (rep % 2) + group) * 128
            for lo in range(2):
                piece = part[lo * 128:(lo + 1) * 128].astype(BF16)
                out_ref[2 * (rep // 2) + lo, start:start + 128, :] = piece


def weight_grads_a(src_t, dq, dk, dv):
    return pl.pallas_call(
        weight_grad_a_kernel,
        grid=(1,),
        in_specs=[
            pl.BlockSpec((1024, 1024), lambda i: (0, 0)),
            pl.BlockSpec((512, 256), lambda i: (0, 0)),
            pl.BlockSpec((1024, 512), lambda i: (0, 0)),
            pl.BlockSpec((1024, 256), lambda i: (0, 1)),
        ],
        out_specs=pl.BlockSpec((4, 256, 1024), lambda i: (0, 0, 0)),
        out_shape=jax.ShapeDtypeStruct((4, 256, 1024), BF16),
        compiler_params=PARAMS,
        cost_estimate=pl.CostEstimate(flops=2 * 1024 * 1024 * 900, bytes_accessed=6 << 20, transcendentals=0),
    )(src_t, dq, dk, dv)


def weight_grads_c(src_t, dq, dv, att_t, cot):
    return pl.pallas_call(
        weight_grad_c_kernel,
        grid=(1,),
        in_specs=[
            pl.BlockSpec((1024, 1024), lambda i: (0, 0)),
            pl.BlockSpec((512, 256), lambda i: (0, 1)),
            pl.BlockSpec((1024, 256), lambda i: (0, 0)),
            pl.BlockSpec((512, 512), lambda i: (0, 0)),
            pl.BlockSpec((512, 1024), lambda i: (0, 0)),
        ],
        out_specs=pl.BlockSpec((4, 1024, 256), lambda i: (0, 0, 0)),
        out_shape=jax.ShapeDtypeStruct((4, 1024, 256), BF16),
        compiler_params=PARAMS,
        cost_estimate=pl.CostEstimate(flops=2 * 1024 * 1024 * 640, bytes_accessed=6 << 20, transcendentals=0),
    )(src_t, dq, dv, att_t, cot)


def regroup(value, names, groups):
    return lax.all_to_all(value, names, 0, 0, axis_index_groups=groups, tiled=True)


def after(value, *events):
    return lax.optimization_barrier((value,) + events)[0]


def chunks(value, here):
    return [
        lax.dynamic_index_in_dim(value, lax.rem(here + step, 4), 0, keepdims=False) for step in (0, 1, 3, 2)
    ]


def spread_sum(pieces, target, *events):
    out = pieces[0].astype(F32)
    came = [
        move(piece, lambda y, x, z, c, step=step: target(step, y, x, z, c))
        for step, piece in zip((1, 3, 2), pieces[1:])
    ]
    for piece in came:
        out = out + after(piece, *events).astype(F32)
    return out.astype(BF16)


def along_y(step, y, x, z, c):
    return (y + step, x, z, c)


def along_x(step, y, x, z, c):
    return (y, x + step, z, c)


ALL_Y, ALL_X, ALL_Z, ALL_C = range(NY), range(NX), range(NZ), range(2)
Z_GROUPS = [[ring * NZ + z for z in ALL_Z] for ring in range(8)]
XC_GROUPS = [
    [flat(y, 2 * xh + xl, z, c) for xl in range(2) for xh in range(2) for c in ALL_C] for y in ALL_Y for z in ALL_Z
]


def next_ring(y, x, z, c):
    ring = 2 * y + x % 2 + 1
    return None if ring == 8 else (ring // 2, (x // 2) * 2 + ring % 2, z, c)


def last_ring(y, x, z, c):
    ring = 2 * y + x % 2 - 1
    return None if ring < 0 else (ring // 2, (x // 2) * 2 + ring % 2, z, c)


def body(inputs, upstream, qkv_weight, out_weight):
    at = lax.axis_index("seq")
    rep = lax.axis_index("rep")
    core = lax.rem(rep, 2)
    ring = at // NZ
    y = ring // 2
    x = 2 * (rep // 2) + lax.rem(ring, 2)
    first = core == 0
    left = rep // 2 == 0

    def in_order(mine, other, axis):
        return jnp.concatenate([jnp.where(first, mine, other), jnp.where(first, other, mine)], axis=axis)

    def groups_of(out, core):
        out = out.reshape(4, 256, 256)
        return jnp.concatenate(
            [lax.dynamic_index_in_dim(out, core, 0, False), lax.dynamic_index_in_dim(out, 2 + core, 0, False)],
            axis=0,
        )

    def across(y, x, z, c):
        return (y, 3 - x, z, c)

    cross = jnp.concatenate(
        [
            lax.dynamic_slice_in_dim(qkv_weight, y * 256, 256, 0),
            lax.dynamic_slice_in_dim(out_weight, y * 256, 256, 0),
        ],
        axis=1,
    )
    cross = move(cross, across)
    far_rows = jnp.zeros((1024, 1024), BF16)
    far_rows = lax.dynamic_update_slice_in_dim(far_rows, cross, y * 256, 0)
    for step in (1, 3, 2):
        piece = move(cross, lambda y, x, z, c, step=step: (y + step, x, z, c))
        far_rows = lax.dynamic_update_slice_in_dim(far_rows, piece, lax.rem(y + 4 - step, 4) * 256, 0)

    def to_give(qkv, out):
        return jnp.concatenate([qkv[:, 256:512], groups_of(out, 1 - core)], axis=0)

    def to_keep(qkv, out):
        return jnp.concatenate([qkv[:, :256], qkv[:, 512:768], groups_of(out, core)], axis=0)

    near = to_keep(qkv_weight, out_weight)
    far = to_keep(far_rows, far_rows[:, 768:])
    near_swap = other_core(to_give(qkv_weight, out_weight))
    far_swap = other_core(to_give(far_rows, far_rows[:, 768:]))

    def to_chips(tokens):
        low, high = tokens[..., :512], tokens[..., 512:]
        other = other_core(jnp.where(first, high, low))
        mixed = in_order(jnp.where(first, low, high), other, 0)
        return regroup(mixed, "seq", Z_GROUPS).reshape(NZ * 64, 512)

    src = to_chips(inputs[0])
    halo = move(src, next_ring)
    cot = to_chips(upstream[0])
    src = jnp.concatenate([halo, src], axis=0)
    src = in_order(src, other_core(src), 1)
    cot = in_order(cot, other_core(cot), 1)

    lo, hi = jnp.where(left, near, far), jnp.where(left, far, near)
    lo_swap, hi_swap = jnp.where(left, near_swap, far_swap), jnp.where(left, far_swap, near_swap)
    weight = jnp.concatenate(
        [
            jnp.where(first, lo[:1024], lo_swap[:1024]),
            jnp.where(first, lo[1024:2048], lo[:1024]),
            jnp.where(first, lo_swap[:1024], lo[1024:2048]),
            jnp.where(first, hi[:1024], hi_swap[:1024]),
            jnp.where(first, hi[1024:2048], hi[:1024]),
            jnp.where(first, hi_swap[:1024], hi[1024:2048]),
        ],
        axis=1,
    )
    weight_o = jnp.concatenate(
        [in_order(lo[2048:], lo_swap[1024:], 1), in_order(hi[2048:], hi_swap[1024:], 1)], axis=1
    )
    src_t = src.T

    qkv = mm(src, weight, 1, 0).astype(BF16)
    g = mm(cot, weight_o, 1, 1).astype(BF16)
    bias = jnp.where(ring == 0, -jnp.inf, 0.0).astype(F32).reshape(1, 1)
    dq, att_t, dk, dv = attention(after(bias, src_t), qkv, g)

    def core_sum(value):
        mine = lax.dynamic_index_in_dim(value, core, 0, keepdims=False)
        other = other_core(lax.dynamic_index_in_dim(value, 1 - core, 0, keepdims=False))
        return mine.astype(F32) + other.astype(F32)

    ig_halo = token_grad(0, weight, None, dk, dv)

    part_a = chunks(weight_grads_a(src_t, dq, after(dk, ig_halo), dv), y)
    ig_halo = core_sum(ig_halo).astype(BF16)
    returned = move(ig_halo, last_ring)

    part_c = chunks(weight_grads_c(src_t, after(dq, ig_halo, *part_a), dv, att_t, cot), x)
    ig = token_grad(1, weight, after(dq, *part_c), dk, dv)
    part_a = spread_sum(part_a, along_y, ig)
    part_c = spread_sum(part_c, along_x, ig)

    ig = (core_sum(ig) + returned.astype(F32)).astype(BF16).reshape(8, 64, 512)
    ig = regroup(ig, "seq", Z_GROUPS).reshape(2, 4, 64, 512)
    part_a = after(part_a, ig)
    kept = lax.dynamic_index_in_dim(ig, core, 0, keepdims=False)
    came = other_core(lax.dynamic_index_in_dim(ig, 1 - core, 0, keepdims=False))
    input_grad = in_order(kept, came, -1)[None]

    part_a = part_a.reshape(2, 128, 4, 256).transpose(0, 2, 1, 3).reshape(8, 128, 256)
    part_a = regroup(part_a, BOTH, XC_GROUPS).reshape(4, 2, 128, 256)
    part_a = jnp.sum(part_a.astype(F32), axis=0).astype(BF16)

    part_o = part_c[512:].reshape(2, 2, 1, 128, 256)
    mine = lax.dynamic_index_in_dim(part_o, core, 0, keepdims=False)
    other = other_core(lax.dynamic_index_in_dim(part_o, 1 - core, 0, keepdims=False))
    part_o = in_order(mine, other, 1).reshape(4, 128, 256)
    part_c = jnp.concatenate([part_c[:512].reshape(4, 128, 256), part_o], axis=1)
    part_c = spread_sum(chunks(part_c, y), along_y).reshape(2, 128, 256)

    last = jnp.concatenate([part_a, part_c], axis=0).reshape(4, 8, 16, 256).transpose(1, 0, 2, 3)
    last = jnp.sum(regroup(last, "seq", Z_GROUPS).astype(F32), axis=0)
    qkv_grad = jnp.where(
        first,
        jnp.concatenate([last[0], last[1], last[2]], axis=1),
        jnp.concatenate([last[2], last[0], last[1]], axis=1),
    )
    return input_grad, qkv_grad, last[3]


def solution(mesh):
    return jax.shard_map(
        body,
        mesh=mesh,
        in_specs=(
            P("rep", None, "seq", None),
            P("rep", None, "seq", None),
            P(None, "rep"),
            P(None, "rep"),
        ),
        out_specs=(P("rep", None, "seq", None), P("seq", "rep"), P("seq", "rep")),
        check_vma=False,
    )
```

```python
import jax
import jax.numpy as jnp
from jax import lax
from jax.experimental import pallas as pl
from jax.experimental.pallas import tpu as pltpu
from jax.sharding import PartitionSpec as P

D = 1024
HEADS = 16
HD = 64
WINDOW = 512
NY, NX, NZ = 4, 4, 8
BOTH = ("seq", "rep")
BF16 = jnp.bfloat16
F32 = jnp.float32
LOG2E = 1.4426950408889634
PARAMS = pltpu.CompilerParams(vmem_limit_bytes=48 * 1024 * 1024)


def flat(y, x, z, c):
    y, x, z = y % NY, x % NX, z % NZ
    return ((y * 2 + x % 2) * NZ + z) * 4 + (x // 2) * 2 + c


PLACES = [(y, x, z, c) for y in range(NY) for x in range(NX) for z in range(NZ) for c in range(2)]


def move(value, target):
    pairs = []
    for place in PLACES:
        goal = target(*place)
        if goal is not None:
            pairs.append((flat(*place), flat(*goal)))
    return lax.ppermute(value, BOTH, pairs)


def other_core(value):
    return move(value, lambda y, x, z, c: (y, x, z, 1 - c))


def mm(a, b, ca, cb):
    return lax.dot_general(a, b, (((ca,), (cb,)), ((), ())), preferred_element_type=F32)


def attention_kernel(bias_ref, q_ref, g_ref, k_ref, v_ref, dq_ref, att_ref, dk_ref, dv_ref):
    size = 256
    bias = bias_ref[0, 0]
    low = lax.broadcasted_iota(jnp.int32, (1, 2 * HD), 1) < HD
    upper = (
        lax.broadcasted_iota(jnp.int32, (size, size), 0) > lax.broadcasted_iota(jnp.int32, (size, size), 1)
    )
    upper_low = jnp.where(upper, 1.0, 0.0).astype(BF16)
    factor = LOG2E * HD ** -0.5
    tiles = [slice(i * size, (i + 1) * size) for i in range(4)]
    keys = [k_ref[tile, :] for tile in tiles]
    vals = [v_ref[tile, :] for tile in tiles]
    keys_t = [k.T for k in keys]
    vals_t = [v.T for v in vals]
    dk = [None] * 4
    dv = [None] * 4

    def add(total, index, term):
        total[index] = term if total[index] is None else total[index] + term

    for block in range(2):
        rows = tiles[block]
        q_pair = q_ref[rows, :]
        g_pair = g_ref[rows, :]
        g_t = g_pair.T.astype(F32)
        dq_t = []
        for head in range(2):
            mine = low if head == 0 else jnp.logical_not(low)
            lanes = slice(head * HD, (head + 1) * HD)
            q = jnp.where(mine, q_pair, jnp.zeros_like(q_pair))
            g = jnp.where(mine, g_pair, jnp.zeros_like(g_pair))
            s0, s1, s2 = [mm(keys[block + i], q, 1, 1) for i in range(3)]
            edge = jnp.where(upper, s0 + bias, s2)
            if block == 0:
                s1 = s1 + bias
            top = jnp.maximum(
                jnp.max(edge, axis=0, keepdims=True), jnp.max(s1, axis=0, keepdims=True)
            )
            edge = jnp.exp2((edge - top) * factor)
            full = jnp.exp2((s1 - top) * factor)
            scale = 1.0 / (jnp.sum(edge, axis=0, keepdims=True) + jnp.sum(full, axis=0, keepdims=True))
            edge = edge * scale
            full = full * scale
            edge_low = edge.astype(BF16)
            p0 = edge_low * upper_low
            p1 = full.astype(BF16)
            p2 = edge_low - p0
            att = (
                mm(vals_t[block][lanes], p0, 1, 0)
                + mm(vals_t[block + 1][lanes], p1, 1, 0)
                + mm(vals_t[block + 2][lanes], p2, 1, 0)
            )
            delta = jnp.sum(g_t[lanes] * att, axis=0, keepdims=True)
            att_ref[lanes, rows] = att.astype(BF16)
            d0, d1, d2 = [mm(vals[block + i], g, 1, 1) for i in range(3)]
            d_edge = (edge * (jnp.where(upper, d0, d2) - delta)).astype(BF16)
            z0 = d_edge * upper_low
            z1 = (full * (d1 - delta)).astype(BF16)
            z2 = d_edge - z0
            dq_t.append(
                mm(keys_t[block][lanes], z0, 1, 0)
                + mm(keys_t[block + 1][lanes], z1, 1, 0)
                + mm(keys_t[block + 2][lanes], z2, 1, 0)
            )
            for i, (p, z) in enumerate(((p0, z0), (p1, z1), (p2, z2))):
                add(dv, block + i, mm(p, g, 1, 0))
                add(dk, block + i, mm(z, q, 1, 0))
        dq = jnp.concatenate(dq_t, axis=0) * (HD ** -0.5)
        dq_ref[rows, :] = dq.T.astype(BF16)
    for i, tile in enumerate(tiles):
        dk_ref[tile, :] = (dk[i] * (HD ** -0.5)).astype(BF16)
        dv_ref[tile, :] = dv[i].astype(BF16)


def attention(bias, qkv, g):
    tokens, width = g.shape
    pairs = width // (2 * HD)
    own = pl.BlockSpec((tokens, 2 * HD), lambda i: (0, i))
    long = pl.BlockSpec((2 * tokens, 2 * HD), lambda i: (0, i))
    return pl.pallas_call(
        attention_kernel,
        grid=(pairs,),
        in_specs=[
            pl.BlockSpec(memory_space=pltpu.SMEM),
            pl.BlockSpec((tokens, 2 * HD), lambda i: (1, i)),
            own,
            pl.BlockSpec((2 * tokens, 2 * HD), lambda i: (0, pairs + i)),
            pl.BlockSpec((2 * tokens, 2 * HD), lambda i: (0, 2 * pairs + i)),
        ],
        out_specs=[own, pl.BlockSpec((2 * HD, tokens), lambda i: (i, 0)), long, long],
        out_shape=[
            jax.ShapeDtypeStruct((tokens, width), BF16),
            jax.ShapeDtypeStruct((width, tokens), BF16),
            jax.ShapeDtypeStruct((2 * tokens, width), BF16),
            jax.ShapeDtypeStruct((2 * tokens, width), BF16),
        ],
        compiler_params=PARAMS,
        cost_estimate=pl.CostEstimate(
            flops=16 * 768 * 256 * 64 * 12, bytes_accessed=6 * 1024 * 1024, transcendentals=16 * 512 * 256
        ),
    )(bias, qkv, g, qkv, qkv)


def token_grad_kernel(*refs):
    out_ref = refs[-1]
    pairs = [(refs[2 * i], refs[2 * i + 1]) for i in range(len(refs) // 2)]
    for half in range(2):
        cols = slice(half * 512, (half + 1) * 512)
        acc = None
        for grad_ref, weight_ref in pairs:
            term = mm(grad_ref[...], weight_ref[cols, :], 1, 1)
            acc = term if acc is None else acc + term
        out_ref[half] = acc.astype(BF16)


def token_grad(rows, weight, dq, dk, dv):
    whole = pl.BlockSpec((512, 512), lambda i: (0, 0))
    tokens = pl.BlockSpec((512, 512), lambda i: (rows, 0))

    def cols(which):
        return pl.BlockSpec((1024, 512), lambda i: (0, which))

    specs, args = [], []
    if dq is not None:
        specs, args = [whole, cols(0)], [dq, weight]
    return pl.pallas_call(
        token_grad_kernel,
        grid=(1,),
        in_specs=specs + [tokens, cols(1), tokens, cols(2)],
        out_specs=pl.BlockSpec((2, 512, 512), lambda i: (0, 0, 0)),
        out_shape=jax.ShapeDtypeStruct((2, 512, 512), BF16),
        compiler_params=PARAMS,
        cost_estimate=pl.CostEstimate(
            flops=2 * 512 * 1024 * 512 * (len(args) // 2 + 2), bytes_accessed=5 << 20, transcendentals=0
        ),
    )(*args, dk, weight, dv, weight)


def weight_grad_a_kernel(src_ref, dq_ref, dk_ref, dv_ref, out_ref):
    for y in range(4):
        rows = slice(y * 256, (y + 1) * 256)
        out_ref[y, :, :256] = mm(src_ref[rows, 512:], dq_ref[...], 1, 0).astype(BF16)
        out_ref[y, :, 256:768] = mm(src_ref[rows, :], dk_ref[...], 1, 0).astype(BF16)
        out_ref[y, :, 768:] = mm(src_ref[rows, :], dv_ref[...], 1, 0).astype(BF16)


def weight_grad_c_kernel(src_ref, dq_ref, dv_ref, att_ref, cot_ref, out_ref):
    for y in range(4):
        rows = slice(y * 256, (y + 1) * 256)
        parts = (mm(src_ref[rows, 512:], dq_ref[...], 1, 0), mm(src_ref[rows, :], dv_ref[...], 1, 0))
        for hi in range(2):
            for lo in range(2):
                piece = parts[hi][lo * 128:(lo + 1) * 128].astype(BF16)
                out_ref[2 * hi + lo, y * 128:(y + 1) * 128, :] = piece
    for group in range(2):
        for rep in range(4):
            part = mm(att_ref[group * 256:(group + 1) * 256, :], cot_ref[:, rep * 256:(rep + 1) * 256], 1, 0)
            start = 512 + (2 * (rep % 2) + group) * 128
            for lo in range(2):
                piece = part[lo * 128:(lo + 1) * 128].astype(BF16)
                out_ref[2 * (rep // 2) + lo, start:start + 128, :] = piece


def weight_grads_a(src_t, dq, dk, dv):
    return pl.pallas_call(
        weight_grad_a_kernel,
        grid=(1,),
        in_specs=[
            pl.BlockSpec((1024, 1024), lambda i: (0, 0)),
            pl.BlockSpec((512, 256), lambda i: (0, 0)),
            pl.BlockSpec((1024, 512), lambda i: (0, 0)),
            pl.BlockSpec((1024, 256), lambda i: (0, 1)),
        ],
        out_specs=pl.BlockSpec((4, 256, 1024), lambda i: (0, 0, 0)),
        out_shape=jax.ShapeDtypeStruct((4, 256, 1024), BF16),
        compiler_params=PARAMS,
        cost_estimate=pl.CostEstimate(flops=2 * 1024 * 1024 * 900, bytes_accessed=6 << 20, transcendentals=0),
    )(src_t, dq, dk, dv)


def weight_grads_c(src_t, dq, dv, att_t, cot):
    return pl.pallas_call(
        weight_grad_c_kernel,
        grid=(1,),
        in_specs=[
            pl.BlockSpec((1024, 1024), lambda i: (0, 0)),
            pl.BlockSpec((512, 256), lambda i: (0, 1)),
            pl.BlockSpec((1024, 256), lambda i: (0, 0)),
            pl.BlockSpec((512, 512), lambda i: (0, 0)),
            pl.BlockSpec((512, 1024), lambda i: (0, 0)),
        ],
        out_specs=pl.BlockSpec((4, 1024, 256), lambda i: (0, 0, 0)),
        out_shape=jax.ShapeDtypeStruct((4, 1024, 256), BF16),
        compiler_params=PARAMS,
        cost_estimate=pl.CostEstimate(flops=2 * 1024 * 1024 * 640, bytes_accessed=6 << 20, transcendentals=0),
    )(src_t, dq, dv, att_t, cot)


def regroup(value, names, groups):
    return lax.all_to_all(value, names, 0, 0, axis_index_groups=groups, tiled=True)


def after(value, *events):
    return lax.optimization_barrier((value,) + events)[0]


def chunks(value, here):
    return [
        lax.dynamic_index_in_dim(value, lax.rem(here + step, 4), 0, keepdims=False) for step in (0, 1, 3, 2)
    ]


def spread_sum(pieces, target, *events):
    out = pieces[0].astype(F32)
    came = [
        move(piece, lambda y, x, z, c, step=step: target(step, y, x, z, c))
        for step, piece in zip((1, 3, 2), pieces[1:])
    ]
    for piece in came:
        out = out + after(piece, *events).astype(F32)
    return out.astype(BF16)


def along_y(step, y, x, z, c):
    return (y + step, x, z, c)


def along_x(step, y, x, z, c):
    return (y, x + step, z, c)


ALL_Y, ALL_X, ALL_Z, ALL_C = range(NY), range(NX), range(NZ), range(2)
Z_GROUPS = [[ring * NZ + z for z in ALL_Z] for ring in range(8)]
XC_GROUPS = [
    [flat(y, 2 * xh + xl, z, c) for xl in range(2) for xh in range(2) for c in ALL_C] for y in ALL_Y for z in ALL_Z
]


def next_ring(y, x, z, c):
    ring = 2 * y + x % 2 + 1
    return None if ring == 8 else (ring // 2, (x // 2) * 2 + ring % 2, z, c)


def last_ring(y, x, z, c):
    ring = 2 * y + x % 2 - 1
    return None if ring < 0 else (ring // 2, (x // 2) * 2 + ring % 2, z, c)


def body(inputs, upstream, qkv_weight, out_weight):
    at = lax.axis_index("seq")
    rep = lax.axis_index("rep")
    core = lax.rem(rep, 2)
    ring = at // NZ
    y = ring // 2
    x = 2 * (rep // 2) + lax.rem(ring, 2)
    first = core == 0
    left = rep // 2 == 0

    def in_order(mine, other, axis):
        return jnp.concatenate([jnp.where(first, mine, other), jnp.where(first, other, mine)], axis=axis)

    def groups_of(out, core):
        out = out.reshape(4, 256, 256)
        return jnp.concatenate(
            [lax.dynamic_index_in_dim(out, core, 0, False), lax.dynamic_index_in_dim(out, 2 + core, 0, False)],
            axis=0,
        )

    def across(y, x, z, c):
        return (y, 3 - x, z, c)

    cross = jnp.concatenate(
        [
            lax.dynamic_slice_in_dim(qkv_weight, y * 256, 256, 0),
            lax.dynamic_slice_in_dim(out_weight, y * 256, 256, 0),
        ],
        axis=1,
    )
    cross = move(cross, across)
    far_rows = jnp.zeros((1024, 1024), BF16)
    far_rows = lax.dynamic_update_slice_in_dim(far_rows, cross, y * 256, 0)
    for step in (1, 3, 2):
        piece = move(cross, lambda y, x, z, c, step=step: (y + step, x, z, c))
        far_rows = lax.dynamic_update_slice_in_dim(far_rows, piece, lax.rem(y + 4 - step, 4) * 256, 0)

    def to_give(qkv, out):
        return jnp.concatenate([qkv[:, 256:512], groups_of(out, 1 - core)], axis=0)

    def to_keep(qkv, out):
        return jnp.concatenate([qkv[:, :256], qkv[:, 512:768], groups_of(out, core)], axis=0)

    near = to_keep(qkv_weight, out_weight)
    far = to_keep(far_rows, far_rows[:, 768:])
    near_swap = other_core(to_give(qkv_weight, out_weight))
    far_swap = other_core(to_give(far_rows, far_rows[:, 768:]))

    def to_chips(tokens):
        low, high = tokens[..., :512], tokens[..., 512:]
        other = other_core(jnp.where(first, high, low))
        mixed = in_order(jnp.where(first, low, high), other, 0)
        return regroup(mixed, "seq", Z_GROUPS).reshape(NZ * 64, 512)

    src = to_chips(inputs[0])
    halo = move(src, next_ring)
    cot = to_chips(upstream[0])
    src = jnp.concatenate([halo, src], axis=0)
    src = in_order(src, other_core(src), 1)
    cot = in_order(cot, other_core(cot), 1)

    lo, hi = jnp.where(left, near, far), jnp.where(left, far, near)
    lo_swap, hi_swap = jnp.where(left, near_swap, far_swap), jnp.where(left, far_swap, near_swap)
    weight = jnp.concatenate(
        [
            jnp.where(first, lo[:1024], lo_swap[:1024]),
            jnp.where(first, lo[1024:2048], lo[:1024]),
            jnp.where(first, lo_swap[:1024], lo[1024:2048]),
            jnp.where(first, hi[:1024], hi_swap[:1024]),
            jnp.where(first, hi[1024:2048], hi[:1024]),
            jnp.where(first, hi_swap[:1024], hi[1024:2048]),
        ],
        axis=1,
    )
    weight_o = jnp.concatenate(
        [in_order(lo[2048:], lo_swap[1024:], 1), in_order(hi[2048:], hi_swap[1024:], 1)], axis=1
    )
    src_t = src.T

    qkv = mm(src, weight, 1, 0).astype(BF16)
    g = mm(cot, weight_o, 1, 1).astype(BF16)
    bias = jnp.where(ring == 0, -jnp.inf, 0.0).astype(F32).reshape(1, 1)
    dq, att_t, dk, dv = attention(bias, qkv, g)

    def core_sum(value):
        mine = lax.dynamic_index_in_dim(value, core, 0, keepdims=False)
        other = other_core(lax.dynamic_index_in_dim(value, 1 - core, 0, keepdims=False))
        return mine.astype(F32) + other.astype(F32)

    ig_halo = token_grad(0, weight, None, dk, dv)

    part_a = chunks(weight_grads_a(src_t, dq, after(dk, ig_halo), dv), y)
    ig_halo = core_sum(ig_halo).astype(BF16)
    returned = move(ig_halo, last_ring)

    part_c = chunks(weight_grads_c(src_t, after(dq, ig_halo, *part_a), dv, att_t, cot), x)
    ig = token_grad(1, weight, after(dq, *part_c), dk, dv)
    part_a = spread_sum(part_a, along_y, ig)
    part_c = spread_sum(part_c, along_x, ig)

    ig = (core_sum(ig) + returned.astype(F32)).astype(BF16).reshape(8, 64, 512)
    ig = regroup(ig, "seq", Z_GROUPS).reshape(2, 4, 64, 512)
    part_a = after(part_a, ig)
    kept = lax.dynamic_index_in_dim(ig, core, 0, keepdims=False)
    came = other_core(lax.dynamic_index_in_dim(ig, 1 - core, 0, keepdims=False))
    input_grad = in_order(kept, came, -1)[None]

    part_a = part_a.reshape(2, 128, 4, 256).transpose(0, 2, 1, 3).reshape(8, 128, 256)
    part_a = regroup(part_a, BOTH, XC_GROUPS).reshape(4, 2, 128, 256)
    part_a = jnp.sum(part_a.astype(F32), axis=0).astype(BF16)

    part_o = part_c[512:].reshape(2, 2, 1, 128, 256)
    mine = lax.dynamic_index_in_dim(part_o, core, 0, keepdims=False)
    other = other_core(lax.dynamic_index_in_dim(part_o, 1 - core, 0, keepdims=False))
    part_o = in_order(mine, other, 1).reshape(4, 128, 256)
    part_c = jnp.concatenate([part_c[:512].reshape(4, 128, 256), part_o], axis=1)
    part_c = spread_sum(chunks(part_c, y), along_y).reshape(2, 128, 256)

    last = jnp.concatenate([part_a, part_c], axis=0).reshape(4, 8, 16, 256).transpose(1, 0, 2, 3)
    last = jnp.sum(regroup(last, "seq", Z_GROUPS).astype(F32), axis=0)
    qkv_grad = jnp.where(
        first,
        jnp.concatenate([last[0], last[1], last[2]], axis=1),
        jnp.concatenate([last[2], last[0], last[1]], axis=1),
    )
    return input_grad, qkv_grad, last[3]


def solution(mesh):
    return jax.shard_map(
        body,
        mesh=mesh,
        in_specs=(
            P("rep", None, "seq", None),
            P("rep", None, "seq", None),
            P(None, "rep"),
            P(None, "rep"),
        ),
        out_specs=(P("rep", None, "seq", None), P("seq", "rep"), P("seq", "rep")),
        check_vma=False,
    )
```
